32 devices in a mesh: sec: 2 (over x), gy: 4 (over z), gx: 4 (over y, core).
Axes of the slice: x: 2, y: 2, z: 4, core: 2. Of those that a mesh axis runs over, the one named last changes fastest.
Arguments:
- fields: float32 [2, 4, 1, 768, 1536], P('sec', None, None, 'gy', 'gx'), may hold values from -6 to 6
- forcing: bfloat16 [2, 4, 1, 768, 1536], P('sec', None, None, 'gy', 'gx'), may hold values from -4 to 4
- courant: float32 [2, 1], replicated, may hold values from -0.18 to 0.18
- diffusion: float32 [4], replicated, may hold values from 0.03 to 0.08
- nest_patch: int32 [4, 4], replicated, may hold values from 0 to 35, as said below
Outputs:
- fields_out: float32 [2, 4, 1, 768, 1536], P('sec', None, None, 'gy', 'gx')
The draws below stay inside these ranges and needn't reach their ends.
Inputs may be any that keep to these rules, and one draw needn't show every extreme that they name: Entry [i, j] names a patch of the parent device in row nest_patch[i, j] // 9 of device column j: patch row (nest_patch[i, j] % 9) // 3 and patch column nest_patch[i, j] % 3 of its 3 x 3 patches. That device row differs from i by at most one. Nests of one column lie on distinct patches; in every column some parent device lies under exactly three nests, and none under more.
All inputs are finite; a program needn't handle non-finite values.
Results may differ from the reference program's by a relative error of at most 0.0003.
Values sent between devices are 32-bit elements; how exact they have to be, the bound alone decides.
A program may use at most 128 MiB of HBM per device.

```python
import math
import jax
import jax.numpy as jnp
from jax import lax

NVAR = 4
LEV = 1
CY = 192
CX = 384
NEST_ROWS = 4
NEST_COLS = 4
NY = 768
NX = 1536


def place_value(order, wanted):
    position = jnp.arange(9, dtype=jnp.int32)
    current = order[1]
    return jnp.where(order == wanted, current, jnp.where(position == 1, wanted, order)).astype(jnp.int32)


def draw_nest_patch(key, part):
    first_key, second_key, third_key = jax.random.split(key, 3)
    offsets = jax.random.randint(first_key, (NEST_ROWS, NEST_COLS), -1, 2)
    offsets = offsets.at[NEST_ROWS - 1, 0].set(0)
    offsets = offsets.at[0, 1].set(0)
    row_index = jnp.arange(NEST_ROWS, dtype=jnp.int32)[:, None]
    target = jnp.clip(row_index + offsets, 0, NEST_ROWS - 1)
    storm = jax.random.randint(second_key, (NEST_COLS,), 1, NEST_ROWS - 1)
    storm = storm.at[0].set(1)
    storm = storm.at[1].set(NEST_ROWS - 2)
    nearby = jnp.abs(row_index - storm[None, :]) <= 1
    target = jnp.where(nearby, storm[None, :], target)
    role = row_index - target + 1
    slot_keys = jax.random.split(third_key, NEST_ROWS * NEST_COLS)
    orders = jax.vmap(lambda single: jax.random.permutation(single, 9))(slot_keys)
    orders = orders.reshape(NEST_ROWS, NEST_COLS, 9).astype(jnp.int32)
    orders = orders.at[NEST_ROWS - 1, 0].set(place_value(orders[NEST_ROWS - 1, 0], 8))
    orders = orders.at[0, 1].set(place_value(orders[0, 1], 0))
    column_index = jnp.arange(NEST_COLS, dtype=jnp.int32)[None, :]
    slot = orders[target, column_index, role]
    return (target * 9 + slot).astype(jnp.int32)


def level_of(own_key, dims, pieces, least, largest):
    loudness, own = 1.0, jax.random.fold_in(own_key, 6)
    for dim, blocks in pieces:
        heights = jnp.exp(jax.random.uniform(jax.random.fold_in(own, dim), (blocks,), jnp.float32, least / len(pieces), largest / len(pieces)))
        loudness = loudness * jnp.repeat(heights, dims[dim] // blocks).reshape([-1 if axis == dim else 1 for axis in range(len(dims))])
    return loudness


def centred(stream_key, dims, scale, reach, shards=(), kind=jnp.bfloat16):
    values = jax.random.normal(stream_key, dims, jnp.float32) * scale
    if len(shards) > 0:
        values = level_of(stream_key, dims, shards, -0.22, 0.18) * values
    return jnp.clip(values, min=-reach, max=reach).astype(kind)


def setup_inputs(seed: int = 0) -> dict:
    key_list = jax.random.split(jax.random.key(seed), 6)
    return {
        "fields": centred(key_list[0], (2, NVAR, LEV, NY, NX), 1.0, 6.0, ((0, 2), (3, 4), (4, 4)), jnp.float32),
        "forcing": centred(key_list[1], (2, NVAR, LEV, NY, NX), 0.3, 4.0, ((0, 2), (3, 4), (4, 4))),
        "courant": jnp.clip(jax.random.uniform(key_list[2], (2, LEV), jnp.float32, -0.18, 0.18), -0.18, 0.18),
        "diffusion": jnp.clip(jnp.exp(jax.random.uniform(key_list[3], (NVAR,), jnp.float32, math.log(0.03), math.log(0.08))), 0.03, 0.08),
        "nest_patch": draw_nest_patch(jax.random.fold_in(key_list[5], 71), 0),
    }


third = 1.0 / 3.0
two_thirds = 2.0 / 3.0


def as_index(value):
    return jnp.asarray(value, dtype=jnp.int32)


def stencil(padded, centre, courant, diffusion, drive):
    eastern = padded[..., 1:-1, 2:]
    western = padded[..., 1:-1, :-2]
    southern = padded[..., 2:, 1:-1]
    northern = padded[..., :-2, 1:-1]
    along_columns = courant[0].reshape(1, -1, 1, 1)
    along_rows = courant[1].reshape(1, -1, 1, 1)
    spread = diffusion.reshape(-1, 1, 1, 1)
    return (centre - 0.5 * along_columns * (eastern - western) - 0.5 * along_rows * (southern - northern)
            + spread * (eastern + western + southern + northern - 4.0 * centre) + drive)


def refine_edge(parent_rim):
    lower_part = parent_rim[..., :-2]
    centre_part = parent_rim[..., 1:-1]
    upper_part = parent_rim[..., 2:]
    first_third = third * lower_part + two_thirds * centre_part
    last_third = two_thirds * centre_part + third * upper_part
    stacked = jnp.stack([first_third, centre_part, last_third], axis=-1)
    return stacked.reshape(parent_rim.shape[:-1] + (3 * (parent_rim.shape[-1] - 2),))


def pack_rims(padded, row_start, col_start, patch_rows, patch_cols):
    field_count = padded.shape[0]
    level_count = padded.shape[1]
    zero = as_index(0)
    row_start = as_index(row_start)
    col_start = as_index(col_start)
    upper = lax.dynamic_slice(padded, (zero, zero, row_start, as_index(col_start + 1)), (field_count, level_count, 1, patch_cols))[:, :, 0]
    lower = lax.dynamic_slice(padded, (zero, zero, as_index(row_start + patch_rows + 1), as_index(col_start + 1)), (field_count, level_count, 1, patch_cols))[:, :, 0]
    western = lax.dynamic_slice(padded, (zero, zero, row_start, col_start), (field_count, level_count, patch_rows + 2, 1))[..., 0]
    eastern = lax.dynamic_slice(padded, (zero, zero, row_start, as_index(col_start + patch_cols + 1)), (field_count, level_count, patch_rows + 2, 1))[..., 0]
    lane_pad = ((0, 0), (0, 0), (0, patch_cols - patch_rows - 2))
    return jnp.stack([upper, lower, jnp.pad(western, lane_pad), jnp.pad(eastern, lane_pad)], axis=2)


def unpack(message, patch_rows):
    upper_row = jnp.concatenate([message[..., 2, 0:1], message[..., 0, :], message[..., 3, 0:1]], axis=-1)
    lower_row = jnp.concatenate([message[..., 2, patch_rows + 1:patch_rows + 2], message[..., 1, :],
                                 message[..., 3, patch_rows + 1:patch_rows + 2]], axis=-1)
    western = message[..., 2, :patch_rows + 2]
    eastern = message[..., 3, :patch_rows + 2]
    return refine_edge(upper_row), refine_edge(lower_row), refine_edge(western), refine_edge(eastern)


def border(field, upper, lower, western, eastern):
    stacked_rows = jnp.concatenate([upper[..., None, :], field, lower[..., None, :]], axis=-2)
    corner_zero = jnp.zeros(western.shape[:-1] + (1,), field.dtype)
    west_column = jnp.concatenate([corner_zero, western, corner_zero], axis=-1)
    east_column = jnp.concatenate([corner_zero, eastern, corner_zero], axis=-1)
    return jnp.concatenate([west_column[..., None], stacked_rows, east_column[..., None]], axis=-1)


def nest_steps(field, drive_fine, edges_start, edges_end, courant, diffusion):
    fine_spread = diffusion * 3.0
    fine_force = drive_fine.astype(jnp.float32) / 3.0
    for substep in range(3):
        fraction = substep / 3.0
        upper, lower, western, eastern = [start_edge + fraction * (end_edge - start_edge)
                                          for start_edge, end_edge in zip(edges_start, edges_end)]
        padded = border(field, upper, lower, western, eastern)
        field = stencil(padded, field, courant, fine_spread, fine_force)
    return field


def reference(fields, forcing, courant, diffusion, nest_patch):
    parent = fields[0]
    nest_all = fields[1]
    nest_drive = forcing[1]
    patch_rows = CY // 3
    patch_cols = CX // 3
    margin = ((0, 0), (0, 0), (1, 1), (1, 1))
    padded_before = jnp.pad(parent, margin)
    advanced = stencil(padded_before, parent, courant, diffusion, forcing[0].astype(jnp.float32))
    padded_after = jnp.pad(advanced, margin)

    def one_nest(flat):
        flat = as_index(flat)
        nest_row = as_index(flat // NEST_COLS)
        nest_col = as_index(flat % NEST_COLS)
        code = as_index(nest_patch[nest_row, nest_col])
        owner = as_index(code // 9)
        slot = as_index(code % 9)
        row_start = as_index(owner * CY + (slot // 3) * patch_rows)
        col_start = as_index(nest_col * CX + (slot % 3) * patch_cols)
        message = jnp.stack([pack_rims(padded_before, row_start, col_start, patch_rows, patch_cols),
                             pack_rims(padded_after, row_start, col_start, patch_rows, patch_cols)], axis=2)
        zero = as_index(0)
        tile_row = as_index(nest_row * CY)
        tile_col = as_index(nest_col * CX)
        own_field = lax.dynamic_slice(nest_all, (zero, zero, tile_row, tile_col), (NVAR, LEV, CY, CX))
        own_drive = lax.dynamic_slice(nest_drive, (zero, zero, tile_row, tile_col), (NVAR, LEV, CY, CX))
        finished = nest_steps(own_field, own_drive, unpack(message[:, :, 0], patch_rows),
                              unpack(message[:, :, 1], patch_rows), courant, diffusion)
        averaged = finished.reshape(NVAR, LEV, patch_rows, 3, patch_cols, 3).mean(axis=(3, 5))
        target = (owner * 3 + slot // 3) * (3 * NEST_COLS) + nest_col * 3 + slot % 3
        return finished, averaged, as_index(target)

    finished_all, averaged_all, targets = lax.map(one_nest, jnp.arange(NEST_ROWS * NEST_COLS, dtype=jnp.int32))
    blocks = advanced.reshape(NVAR, LEV, 3 * NEST_ROWS, patch_rows, 3 * NEST_COLS, patch_cols)
    blocks = blocks.transpose(2, 4, 0, 1, 3, 5).reshape(9 * NEST_ROWS * NEST_COLS, NVAR, LEV, patch_rows, patch_cols)
    blocks = blocks.at[targets].set(averaged_all)
    corrected = blocks.reshape(3 * NEST_ROWS, 3 * NEST_COLS, NVAR, LEV, patch_rows, patch_cols)
    corrected = corrected.transpose(2, 3, 0, 4, 1, 5).reshape(NVAR, LEV, NY, NX)
    nest_final = finished_all.reshape(NEST_ROWS, NEST_COLS, NVAR, LEV, CY, CX)
    nest_final = nest_final.transpose(2, 3, 0, 4, 1, 5).reshape(NVAR, LEV, NY, NX)
    return jnp.stack([corrected, nest_final])
```

```python
import functools

import jax
import jax.numpy as jnp
from jax import lax
from jax.experimental import pallas as pl
from jax.experimental.pallas import tpu as pltpu
from jax.sharding import PartitionSpec as P

MESH = pl.DeviceIdType.MESH
third = 1.0 / 3.0
PAD_ROWS = 8
LANES = 128
DIRECTIONS = ((-1, 0), (1, 0), (0, -1), (0, 1), (-1, -1), (-1, 1), (1, -1), (1, 1))


def all_of(terms):
    result = terms[0]
    for term in terms[1:]:
        result = jnp.logical_and(result, term)
    return result


def kernel(
    rows_total,
    cols_total,
    fields_hbm,
    forcing_hbm,
    courant,
    diffusion,
    nest_patch,
    out_ref,
    ext,
    force,
    col_send,
    col_recv,
    rim_rows,
    rim_send,
    rim_recv,
    block_send,
    block_recv,
    fold,
    load_sem,
    halo_send_sem,
    halo_recv_sem,
    rim_send_sem,
    rim_recv_sem,
    up_send_sem,
    up_recv_sem,
    side_send_sem,
    side_recv_sem,
):
    count, height, width = out_ref.shape
    patch_rows, patch_cols = height // 3, width // 3
    sec = lax.axis_index("sec")
    row = lax.axis_index("gy")
    col = lax.axis_index("gx")
    is_parent = sec == 0
    is_nest = sec == 1
    top, bottom = PAD_ROWS, PAD_ROWS + height
    left, right = LANES, LANES + width

    load_fields = pltpu.make_async_copy(
        fields_hbm, ext.at[0, :, top:bottom, left:right], load_sem.at[0]
    )
    load_force = pltpu.make_async_copy(forcing_hbm, force, load_sem.at[1])
    load_fields.start()
    load_force.start()

    def there(dy, dx=0):
        terms = []
        if dy < 0:
            terms.append(row > 0)
        if dy > 0:
            terms.append(row < rows_total - 1)
        if dx < 0:
            terms.append(col > 0)
        if dx > 0:
            terms.append(col < cols_total - 1)
        return all_of(terms) if terms else row >= 0

    barrier = pltpu.get_barrier_semaphore()

    def greet(condition, where):
        @pl.when(condition)
        def _():
            pl.semaphore_signal(barrier, inc=1, device_id=where, device_id_type=MESH)

    for dy, dx in DIRECTIONS:
        greet(all_of([is_parent, there(dy, dx)]), (sec, row + dy, col + dx))
    for dy in (-1, 0, 1):
        greet(there(dy), (1 - sec, row + dy, col))
    def one_if(condition):
        return jnp.where(condition, jnp.int32(1), jnp.int32(0))

    in_row = one_if(there(0, -1)) + one_if(there(0, 1)) + 1
    in_column = one_if(there(-1)) + one_if(there(1)) + 1
    pl.semaphore_wait(barrier, in_column + (1 - sec) * (in_row * in_column - 1))
    load_fields.wait()

    lane = lax.broadcasted_iota(jnp.int32, (1, LANES), 1)
    wide_lane = lax.broadcasted_iota(jnp.int32, (1, width), 1)
    half_x = 0.5 * courant[0, 0]
    half_y = 0.5 * courant[1, 0]
    chunk = 32

    def stencil_field(index, source, west_of, east_of, spread, drive_scale, store):
        for start in range(0, height, chunk):
            rows = slice(top + start, top + start + chunk)
            centre = source[rows, left:right]
            north = source[top + start - 1 : top + start - 1 + chunk, left:right]
            south = source[top + start + 1 : top + start + 1 + chunk, left:right]
            west = jnp.where(wide_lane == 0, west_of(start), pltpu.roll(centre, 1, 1))
            east = jnp.where(wide_lane == width - 1, east_of(start), pltpu.roll(centre, width - 1, 1))
            drive = force[index, start : start + chunk].astype(jnp.float32)
            value = (
                (1.0 - 4.0 * spread) * centre
                + (spread - half_x) * east
                + (spread + half_x) * west
                + (spread - half_y) * south
                + (spread + half_y) * north
                + drive_scale * drive
            )
            store(start, value)

    @pl.when(is_parent)
    def _parent():
        def halo_copy(phase, direction):
            dy, dx = DIRECTIONS[direction]
            where = (sec, row + dy, col + dx)
            sems = (halo_send_sem.at[phase, direction], halo_recv_sem.at[phase, direction])
            if dy == 0:
                side = 0 if dx < 0 else 1
                source = col_send.at[phase, side]
                target = col_recv.at[phase, 1 - side]
            else:
                rows_from = slice(top, top + PAD_ROWS) if dy < 0 else slice(bottom - PAD_ROWS, bottom)
                rows_to = slice(bottom, bottom + PAD_ROWS) if dy < 0 else slice(0, top)
                if dx == 0:
                    lanes_from = lanes_to = slice(left, right)
                elif dx < 0:
                    lanes_from, lanes_to = slice(left, left + LANES), slice(right, right + LANES)
                else:
                    lanes_from, lanes_to = slice(right - LANES, right), slice(0, left)
                source = ext.at[phase, :, rows_from, lanes_from]
                target = ext.at[phase, :, rows_to, lanes_to]
            return pltpu.make_async_remote_copy(
                src_ref=source,
                dst_ref=target,
                send_sem=sems[0],
                recv_sem=sems[1],
                device_id=where,
                device_id_type=MESH,
            )

        def start_exchange(phase):
            for direction in (0, 1, 4, 5, 6, 7):

                @pl.when(there(*DIRECTIONS[direction]))
                def _():
                    halo_copy(phase, direction).start()

            packed = jnp.zeros((height, LANES), jnp.float32)
            for index in range(count):
                first = ext[phase, index, top:bottom, left : left + LANES]
                last = ext[phase, index, top:bottom, right - LANES : right]
                packed = jnp.where(lane == index, first[:, 0:1], packed)
                packed = jnp.where(lane == 8 + index, last[:, LANES - 1 : LANES], packed)
            tall = col_send.shape[-1]
            packed = jnp.concatenate([packed, jnp.zeros((tall - height, LANES), jnp.float32)], axis=0)
            flat = packed.T
            col_send[phase, 0] = flat[0:8]
            col_send[phase, 1] = flat[8:16]
            for direction in (2, 3):

                @pl.when(there(*DIRECTIONS[direction]))
                def _():
                    halo_copy(phase, direction).start()

            for direction in range(8):
                dy, dx = DIRECTIONS[direction]

                @pl.when(jnp.logical_not(there(-dy, -dx)))
                def _():
                    if dy == 0:
                        side = 1 if dx < 0 else 0
                        col_recv[phase, side] = jnp.zeros(col_recv.shape[2:], jnp.float32)
                    else:
                        rows_to = slice(bottom, bottom + PAD_ROWS) if dy < 0 else slice(0, top)
                        if dx == 0:
                            lanes_to = slice(left, right)
                        elif dx < 0:
                            lanes_to = slice(right, right + LANES)
                        else:
                            lanes_to = slice(0, left)
                        ext[phase, :, rows_to, lanes_to] = jnp.zeros(
                            (count, PAD_ROWS, lanes_to.stop - lanes_to.start), jnp.float32
                        )

        def end_exchange(phase):
            for direction in range(8):
                dy, dx = DIRECTIONS[direction]

                @pl.when(there(-dy, -dx))
                def _():
                    halo_copy(phase, direction).wait_recv()

            both = jnp.concatenate(
                [
                    col_recv[phase, 0],
                    col_recv[phase, 1],
                    jnp.zeros((LANES - 16, col_recv.shape[-1]), jnp.float32),
                ],
                axis=0,
            )
            columns = both.T
            for index in range(count):
                for side, base in ((0, 0), (1, 8)):
                    value = columns[0:height, base + index : base + index + 1]
                    begin = 0 if side == 0 else right
                    ext[phase, index, top:bottom, begin : begin + LANES] = jnp.broadcast_to(
                        value, (height, LANES)
                    )

        start_exchange(0)
        load_force.wait()
        end_exchange(0)

        def advance(index, carry):
            source = ext.at[0, index]

            def store(start, value):
                ext[1, index, top + start : top + start + chunk, left:right] = value

            stencil_field(
                index,
                source,
                lambda start: source[top + start : top + start + chunk, 0:LANES][:, LANES - 1 : LANES],
                lambda start: source[top + start : top + start + chunk, right : right + LANES][:, 0:1],
                diffusion[index],
                1.0,
                store,
            )
            return carry

        lax.fori_loop(0, count, advance, 0)
        start_exchange(1)
        end_exchange(1)

        def rim_copy(member):
            return pltpu.make_async_remote_copy(
                src_ref=rim_send.at[member],
                dst_ref=rim_recv.at[2 - member],
                send_sem=rim_send_sem.at[member],
                recv_sem=rim_recv_sem.at[2 - member],
                device_id=(1 - sec, row + member - 1, col),
                device_id_type=MESH,
            )

        full = ext.shape[2]
        stretch = 2 * LANES
        packed = jnp.zeros((full, LANES), jnp.float32)
        for index in range(count):
            for phase in range(2):
                place = 2 * index + phase
                for part in range(3):
                    above = top + part * patch_rows - 1
                    below = top + (part + 1) * patch_rows
                    rim_rows[part, place : place + 1] = ext[phase, index, above : above + 1, left:right]
                    rim_rows[part, 8 + place : 9 + place] = ext[phase, index, below : below + 1, left:right]
                    begin = part * patch_cols
                    western = ext[phase, index, :, begin : begin + LANES]
                    begin = left + (part + 1) * patch_cols
                    eastern = ext[phase, index, :, begin : begin + LANES]
                    packed = jnp.where(lane == 16 * part + place, western[:, LANES - 1 : LANES], packed)
                    packed = jnp.where(lane == 16 * part + 8 + place, eastern[:, 0:1], packed)
        packed = jnp.concatenate([packed, jnp.zeros((stretch - full, LANES), jnp.float32)], axis=0)
        flat = packed.T

        def choose(number, options):
            return jnp.where(number == 0, options[0], jnp.where(number == 1, options[1], options[2]))

        for member in range(3):
            target_row = jnp.clip(row + member - 1, 0, rows_total - 1)
            slot = lax.rem(nest_patch[target_row, col], 9)
            slot_row = lax.div(slot, 3)
            slot_col = lax.rem(slot, 3)
            rows = choose(slot_row, [rim_rows[part] for part in range(3)])
            rim_send[member, 0:16] = choose(
                slot_col, [rows[:, part * patch_cols : (part + 1) * patch_cols] for part in range(3)]
            )
            lines = choose(slot_col, [flat[16 * part : 16 * part + 16] for part in range(3)])
            rim_send[member, 16:32] = choose(
                slot_row, [lines[:, part * patch_rows : part * patch_rows + LANES] for part in range(3)]
            )

            @pl.when(there(member - 1))
            def _():
                rim_copy(member).start()

        choice = [jnp.int32(-1)] * 9
        for member in range(3):
            source = row + member - 1
            entry = nest_patch[jnp.clip(source, 0, rows_total - 1), col]
            valid = all_of([source >= 0, source < rows_total, lax.div(entry, 9) == row])
            for slot in range(9):
                choice[slot] = jnp.where(
                    jnp.logical_and(valid, lax.rem(entry, 9) == slot), jnp.int32(member), choice[slot]
                )

        def up_copy(index):
            return pltpu.make_async_remote_copy(
                src_ref=block_send.at[index],
                dst_ref=block_recv.at[1, index],
                send_sem=up_send_sem.at[index],
                recv_sem=up_recv_sem.at[index],
                device_id=(1 - sec, row, col),
                device_id_type=MESH,
            )

        def side_copy(index, step):
            lane_of = 0 if step < 0 else 1
            return pltpu.make_async_remote_copy(
                src_ref=block_recv.at[1, index],
                dst_ref=block_recv.at[1 - step, index],
                send_sem=side_send_sem.at[lane_of, index],
                recv_sem=side_recv_sem.at[lane_of, index],
                device_id=(sec, row + step, col),
                device_id_type=MESH,
            )

        for step in (-1, 1):

            @pl.when(jnp.logical_not(there(-step)))
            def _():
                block_recv[1 - step] = jnp.zeros(block_recv.shape[1:], jnp.float32)

        for index in range(count):
            up_copy(index).wait_recv()
            for step in (-1, 1):

                @pl.when(there(step))
                def _():
                    side_copy(index, step).start()

        for index in range(count):
            for step in (-1, 1):

                @pl.when(there(-step))
                def _():
                    side_copy(index, step).wait_recv()

            for slot in range(9):
                rows = slice((slot // 3) * patch_rows, (slot // 3 + 1) * patch_rows)
                lanes = slice((slot % 3) * patch_cols, (slot % 3 + 1) * patch_cols)
                own = ext[
                    1, index, top + rows.start : top + rows.stop, left + lanes.start : left + lanes.stop
                ]
                block = own
                for member in range(3):
                    block = jnp.where(choice[slot] == member, block_recv[member, index], block)
                out_ref[index, rows, lanes] = block

        for phase in range(2):
            for direction in range(8):

                @pl.when(there(*DIRECTIONS[direction]))
                def _():
                    halo_copy(phase, direction).wait_send()

        for member in range(3):

            @pl.when(there(member - 1))
            def _():
                rim_copy(member).wait_send()

        for index in range(count):
            for step in (-1, 1):

                @pl.when(there(step))
                def _():
                    side_copy(index, step).wait_send()

    @pl.when(is_nest)
    def _nest():
        for member in range(3):

            @pl.when(there(member - 1))
            def _():
                pltpu.make_async_remote_copy(
                    src_ref=rim_send.at[2 - member],
                    dst_ref=rim_recv.at[member],
                    send_sem=rim_send_sem.at[2 - member],
                    recv_sem=rim_recv_sem.at[member],
                    device_id=(1 - sec, row + member - 1, col),
                    device_id_type=MESH,
                ).wait_recv()

            @pl.when(jnp.logical_not(there(member - 1)))
            def _():
                rim_recv[member] = jnp.zeros(rim_recv.shape[1:], jnp.float32)

        pick = lax.div(nest_patch[row, col], 9) - row + 1
        message = rim_recv[0]
        for member in (1, 2):
            message = jnp.where(pick == member, rim_recv[member], message)
        columns = message[16:32]

        def refine_weights(cells, fine, offset):
            nest = lax.broadcasted_iota(jnp.int32, (cells, fine), 1)
            cell = lax.broadcasted_iota(jnp.int32, (cells, fine), 0) - offset
            delta = nest - 3 * cell - 1
            near = jnp.abs(delta)
            value = jnp.where(near == 0, 3, jnp.where(near == 1, 2, jnp.where(near == 2, 1, 0)))
            return value.astype(jnp.float32)

        row_weights = refine_weights(LANES, width, 0)
        col_weights = refine_weights(LANES, height, PAD_ROWS)
        fine_rows = third * jnp.dot(
            message[0:16], row_weights, precision=lax.Precision.HIGHEST, preferred_element_type=jnp.float32
        )

        def corners(rows, at):
            west = columns[0:8, at : at + 1]
            east = columns[8:16, at : at + 1]
            return (
                rows
                + jnp.where(wide_lane == 0, third * west, 0.0)
                + jnp.where(wide_lane == width - 1, third * east, 0.0)
            )

        upper = corners(fine_rows[0:8], PAD_ROWS - 1)
        lower = corners(fine_rows[8:16], PAD_ROWS + patch_rows)
        column_block = jnp.concatenate([columns, jnp.zeros((LANES - 16, LANES), jnp.float32)], axis=0)
        fine_columns = third * jnp.dot(
            column_block, col_weights, precision=lax.Precision.HIGHEST, preferred_element_type=jnp.float32
        )
        tall_pad = jnp.zeros((LANES, col_send.shape[-1] - height), jnp.float32)
        fine_columns = jnp.concatenate([fine_columns, tall_pad], axis=1).T
        load_force.wait()
        averaging = (
            lax.broadcasted_iota(jnp.int32, (width, patch_cols), 0) // 3
            == lax.broadcasted_iota(jnp.int32, (width, patch_cols), 1)
        ).astype(jnp.bfloat16)

        def blend(old, new, substep):
            return old + (substep / 3.0) * (new - old) if substep else old

        for index in range(count):
            spread = 3.0 * diffusion[index]
            for substep in range(3):
                now = substep % 2
                source = ext.at[now, index]
                at = 2 * index
                source[top - 1 : top, left:right] = blend(upper[at : at + 1], upper[at + 1 : at + 2], substep)
                source[bottom : bottom + 1, left:right] = blend(
                    lower[at : at + 1], lower[at + 1 : at + 2], substep
                )
                west = blend(fine_columns[0:height, at : at + 1], fine_columns[0:height, at + 1 : at + 2], substep)
                east = blend(
                    fine_columns[0:height, 8 + at : 9 + at], fine_columns[0:height, 9 + at : 10 + at], substep
                )

                def store(start, value, substep=substep, now=now, index=index):
                    if substep < 2:
                        ext[1 - now, index, top + start : top + start + chunk, left:right] = value
                    else:
                        out_ref[index, start : start + chunk] = value

                stencil_field(
                    index,
                    source,
                    lambda start: west[start : start + chunk],
                    lambda start: east[start : start + chunk],
                    spread,
                    third,
                    store,
                )
            full = out_ref[index]
            high = full.astype(jnp.bfloat16)
            low = (full - high.astype(jnp.float32)).astype(jnp.bfloat16)
            across = jnp.dot(high, averaging, preferred_element_type=jnp.float32) + jnp.dot(
                low, averaging, preferred_element_type=jnp.float32
            )
            fold[...] = across
            block_send[index] = (1.0 / 9.0) * (
                fold[pl.ds(0, patch_rows, stride=3)]
                + fold[pl.ds(1, patch_rows, stride=3)]
                + fold[pl.ds(2, patch_rows, stride=3)]
            )
            pltpu.make_async_remote_copy(
                src_ref=block_send.at[index],
                dst_ref=block_recv.at[1, index],
                send_sem=up_send_sem.at[index],
                recv_sem=up_recv_sem.at[index],
                device_id=(1 - sec, row, col),
                device_id_type=MESH,
            ).start()
        for index in range(count):
            pltpu.make_async_remote_copy(
                src_ref=block_send.at[index],
                dst_ref=block_recv.at[1, index],
                send_sem=up_send_sem.at[index],
                recv_sem=up_recv_sem.at[index],
                device_id=(1 - sec, row, col),
                device_id_type=MESH,
            ).wait_send()


def on_device(fields, forcing, courant, diffusion, nest_patch):
    _, count, levels, height, width = fields.shape
    own = fields.reshape(count, height, width)
    drive = forcing.reshape(count, height, width)
    rows_total = lax.axis_size("gy")
    cols_total = lax.axis_size("gx")
    patch_rows, patch_cols = height // 3, width // 3
    tall = -(-height // LANES) * LANES
    f32 = jnp.float32
    smem = pl.BlockSpec(memory_space=pltpu.SMEM)
    dma = pltpu.SemaphoreType.DMA
    result = pl.pallas_call(
        functools.partial(kernel, rows_total, cols_total),
        out_shape=jax.ShapeDtypeStruct((count, height, width), f32),
        in_specs=[pl.BlockSpec(memory_space=pl.ANY)] * 2 + [smem] * 3,
        out_specs=pl.BlockSpec(memory_space=pltpu.VMEM),
        scratch_shapes=[
            pltpu.VMEM((2, count, height + 2 * PAD_ROWS, width + 2 * LANES), f32),
            pltpu.VMEM((count, height, width), jnp.bfloat16),
            pltpu.VMEM((2, 2, 8, tall), f32),
            pltpu.VMEM((2, 2, 8, tall), f32),
            pltpu.VMEM((3, 16, width), f32),
            pltpu.VMEM((3, 32, LANES), f32),
            pltpu.VMEM((3, 32, LANES), f32),
            pltpu.VMEM((count, patch_rows, patch_cols), f32),
            pltpu.VMEM((3, count, patch_rows, patch_cols), f32),
            pltpu.VMEM((height, patch_cols), f32),
            dma((2,)),
            dma((2, 8)),
            dma((2, 8)),
            dma((3,)),
            dma((3,)),
            dma((count,)),
            dma((count,)),
            dma((2, count)),
            dma((2, count)),
        ],
        compiler_params=pltpu.CompilerParams(
            collective_id=0, has_side_effects=True, vmem_limit_bytes=40 * 1024 * 1024
        ),
    )(own, drive, courant, diffusion, nest_patch)
    return result.reshape(fields.shape)


def solution(mesh):
    return jax.shard_map(
        on_device,
        mesh=mesh,
        in_specs=(
            P("sec", None, None, "gy", "gx"),
            P("sec", None, None, "gy", "gx"),
            P(),
            P(),
            P(),
        ),
        out_specs=P("sec", None, None, "gy", "gx"),
        check_vma=False,
    )
```

```python
import functools

import jax
import jax.numpy as jnp
from jax import lax
from jax.experimental import pallas as pl
from jax.experimental.pallas import tpu as pltpu
from jax.sharding import PartitionSpec as P

MESH = pl.DeviceIdType.MESH
third = 1.0 / 3.0
PAD_ROWS = 8
LANES = 128
DIRECTIONS = ((-1, 0), (1, 0), (0, -1), (0, 1), (-1, -1), (-1, 1), (1, -1), (1, 1))


def all_of(terms):
    result = terms[0]
    for term in terms[1:]:
        result = jnp.logical_and(result, term)
    return result


def kernel(
    rows_total,
    cols_total,
    fields_hbm,
    forcing_hbm,
    courant,
    diffusion,
    nest_patch,
    out_ref,
    ext,
    force,
    col_send,
    col_recv,
    rim_rows,
    rim_send,
    rim_recv,
    block_send,
    block_recv,
    fold,
    load_sem,
    halo_send_sem,
    halo_recv_sem,
    rim_send_sem,
    rim_recv_sem,
    up_send_sem,
    up_recv_sem,
    side_send_sem,
    side_recv_sem,
):
    count, height, width = out_ref.shape
    patch_rows, patch_cols = height // 3, width // 3
    sec = lax.axis_index("sec")
    row = lax.axis_index("gy")
    col = lax.axis_index("gx")
    is_parent = sec == 0
    is_nest = sec == 1
    top, bottom = PAD_ROWS, PAD_ROWS + height
    left, right = LANES, LANES + width

    load_fields = pltpu.make_async_copy(
        fields_hbm, ext.at[0, :, top:bottom, left:right], load_sem.at[0]
    )
    load_force = pltpu.make_async_copy(forcing_hbm, force, load_sem.at[1])
    load_fields.start()
    load_force.start()

    def there(dy, dx=0):
        terms = []
        if dy < 0:
            terms.append(row > 0)
        if dy > 0:
            terms.append(row < rows_total - 1)
        if dx < 0:
            terms.append(col > 0)
        if dx > 0:
            terms.append(col < cols_total - 1)
        return all_of(terms) if terms else row >= 0

    barrier = pltpu.get_barrier_semaphore()

    def greet(condition, where):
        @pl.when(condition)
        def _():
            pl.semaphore_signal(barrier, inc=1, device_id=where, device_id_type=MESH)

    for dy, dx in DIRECTIONS:
        greet(all_of([is_parent, there(dy, dx)]), (sec, row + dy, col + dx))
    for dy in (-1, 0, 1):
        greet(there(dy), (1 - sec, row + dy, col))
    def one_if(condition):
        return jnp.where(condition, jnp.int32(1), jnp.int32(0))

    in_row = one_if(there(0, -1)) + one_if(there(0, 1)) + 1
    in_column = one_if(there(-1)) + one_if(there(1)) + 1
    pl.semaphore_wait(barrier, in_column + (1 - sec) * (in_row * in_column - 1))
    load_fields.wait()

    lane = lax.broadcasted_iota(jnp.int32, (1, LANES), 1)
    wide_lane = lax.broadcasted_iota(jnp.int32, (1, width), 1)
    half_x = 0.5 * courant[0, 0]
    half_y = 0.5 * courant[1, 0]
    chunk = 32

    def stencil_field(index, source, west_of, east_of, spread, drive_scale, store):
        for start in range(0, height, chunk):
            rows = slice(top + start, top + start + chunk)
            centre = source[rows, left:right]
            north = source[top + start - 1 : top + start - 1 + chunk, left:right]
            south = source[top + start + 1 : top + start + 1 + chunk, left:right]
            west = jnp.where(wide_lane == 0, west_of(start), pltpu.roll(centre, 1, 1))
            east = jnp.where(wide_lane == width - 1, east_of(start), pltpu.roll(centre, width - 1, 1))
            drive = force[index, start : start + chunk].astype(jnp.float32)
            value = (
                (1.0 - 4.0 * spread) * centre
                + (spread - half_x) * east
                + (spread + half_x) * west
                + (spread - half_y) * south
                + (spread + half_y) * north
                + drive_scale * drive
            )
            store(start, value)

    @pl.when(is_parent)
    def _parent():
        def halo_copy(phase, direction):
            dy, dx = DIRECTIONS[direction]
            where = (sec, row + dy, col + dx)
            sems = (halo_send_sem.at[phase, direction], halo_recv_sem.at[phase, direction])
            if dy == 0:
                side = 0 if dx < 0 else 1
                source = col_send.at[phase, side]
                target = col_recv.at[phase, 1 - side]
            else:
                rows_from = slice(top, top + PAD_ROWS) if dy < 0 else slice(bottom - PAD_ROWS, bottom)
                rows_to = slice(bottom, bottom + PAD_ROWS) if dy < 0 else slice(0, top)
                if dx == 0:
                    lanes_from = lanes_to = slice(left, right)
                elif dx < 0:
                    lanes_from, lanes_to = slice(left, left + LANES), slice(right, right + LANES)
                else:
                    lanes_from, lanes_to = slice(right - LANES, right), slice(0, left)
                source = ext.at[phase, :, rows_from, lanes_from]
                target = ext.at[phase, :, rows_to, lanes_to]
            return pltpu.make_async_remote_copy(
                src_ref=source,
                dst_ref=target,
                send_sem=sems[0],
                recv_sem=sems[1],
                device_id=where,
                device_id_type=MESH,
            )

        def start_exchange(phase):
            for direction in (0, 1, 4, 5, 6, 7):

                @pl.when(there(*DIRECTIONS[direction]))
                def _():
                    halo_copy(phase, direction).start()

            packed = jnp.zeros((height, LANES), jnp.float32)
            for index in range(count):
                first = ext[phase, index, top:bottom, left : left + LANES]
                last = ext[phase, index, top:bottom, right - LANES : right]
                packed = jnp.where(lane == index, first[:, 0:1], packed)
                packed = jnp.where(lane == 8 + index, last[:, LANES - 1 : LANES], packed)
            tall = col_send.shape[-1]
            packed = jnp.concatenate([packed, jnp.zeros((tall - height, LANES), jnp.float32)], axis=0)
            flat = packed.T
            col_send[phase, 0] = flat[0:8]
            col_send[phase, 1] = flat[8:16]
            for direction in (2, 3):

                @pl.when(there(*DIRECTIONS[direction]))
                def _():
                    halo_copy(phase, direction).start()

            for direction in range(8):
                dy, dx = DIRECTIONS[direction]

                @pl.when(jnp.logical_not(there(-dy, -dx)))
                def _():
                    if dy == 0:
                        side = 1 if dx < 0 else 0
                        col_recv[phase, side] = jnp.zeros(col_recv.shape[2:], jnp.float32)
                    else:
                        rows_to = slice(bottom, bottom + PAD_ROWS) if dy < 0 else slice(0, top)
                        if dx == 0:
                            lanes_to = slice(left, right)
                        elif dx < 0:
                            lanes_to = slice(right, right + LANES)
                        else:
                            lanes_to = slice(0, left)
                        ext[phase, :, rows_to, lanes_to] = jnp.zeros(
                            (count, PAD_ROWS, lanes_to.stop - lanes_to.start), jnp.float32
                        )

        def end_exchange(phase):
            for direction in range(8):
                dy, dx = DIRECTIONS[direction]

                @pl.when(there(-dy, -dx))
                def _():
                    halo_copy(phase, direction).wait_recv()

            both = jnp.concatenate(
                [
                    col_recv[phase, 0],
                    col_recv[phase, 1],
                    jnp.zeros((LANES - 16, col_recv.shape[-1]), jnp.float32),
                ],
                axis=0,
            )
            columns = both.T
            for index in range(count):
                for side, base in ((0, 0), (1, 8)):
                    value = columns[0:height, base + index : base + index + 1]
                    begin = 0 if side == 0 else right
                    ext[phase, index, top:bottom, begin : begin + LANES] = jnp.broadcast_to(
                        value, (height, LANES)
                    )

        start_exchange(0)
        load_force.wait()
        end_exchange(0)

        def advance(index, carry):
            source = ext.at[0, index]

            def store(start, value):
                ext[1, index, top + start : top + start + chunk, left:right] = value

            stencil_field(
                index,
                source,
                lambda start: source[top + start : top + start + chunk, 0:LANES][:, LANES - 1 : LANES],
                lambda start: source[top + start : top + start + chunk, right : right + LANES][:, 0:1],
                diffusion[index],
                1.0,
                store,
            )
            return carry

        lax.fori_loop(0, count, advance, 0)
        start_exchange(1)
        end_exchange(1)

        def rim_copy(member):
            return pltpu.make_async_remote_copy(
                src_ref=rim_send.at[member],
                dst_ref=rim_recv.at[2 - member],
                send_sem=rim_send_sem.at[member],
                recv_sem=rim_recv_sem.at[2 - member],
                device_id=(1 - sec, row + member - 1, col),
                device_id_type=MESH,
            )

        full = ext.shape[2]
        stretch = 2 * LANES
        packed = jnp.zeros((full, LANES), jnp.float32)
        for index in range(count):
            for phase in range(2):
                place = 2 * index + phase
                for part in range(3):
                    above = top + part * patch_rows - 1
                    below = top + (part + 1) * patch_rows
                    rim_rows[part, place : place + 1] = ext[phase, index, above : above + 1, left:right]
                    rim_rows[part, 8 + place : 9 + place] = ext[phase, index, below : below + 1, left:right]
                    begin = part * patch_cols
                    western = ext[phase, index, :, begin : begin + LANES]
                    begin = left + (part + 1) * patch_cols
                    eastern = ext[phase, index, :, begin : begin + LANES]
                    packed = jnp.where(lane == 16 * part + place, western[:, LANES - 1 : LANES], packed)
                    packed = jnp.where(lane == 16 * part + 8 + place, eastern[:, 0:1], packed)
        packed = jnp.concatenate([packed, jnp.zeros((stretch - full, LANES), jnp.float32)], axis=0)
        flat = packed.T

        def choose(number, options):
            return jnp.where(number == 0, options[0], jnp.where(number == 1, options[1], options[2]))

        for member in range(3):
            target_row = jnp.clip(row + member - 1, 0, rows_total - 1)
            slot = lax.rem(nest_patch[target_row, col], 9)
            slot_row = lax.div(slot, 3)
            slot_col = lax.rem(slot, 3)
            rows = choose(slot_row, [rim_rows[part] for part in range(3)])
            rim_send[member, 0:16] = choose(
                slot_col, [rows[:, part * patch_cols : (part + 1) * patch_cols] for part in range(3)]
            )
            lines = choose(slot_col, [flat[16 * part : 16 * part + 16] for part in range(3)])
            rim_send[member, 16:32] = choose(
                slot_row, [lines[:, part * patch_rows : part * patch_rows + LANES] for part in range(3)]
            )

            @pl.when(there(member - 1))
            def _():
                rim_copy(member).start()

        choice = [jnp.int32(-1)] * 9
        for member in range(3):
            source = row + member - 1
            entry = nest_patch[jnp.clip(source, 0, rows_total - 1), col]
            valid = all_of([source >= 0, source < rows_total, lax.div(entry, 9) == row])
            for slot in range(9):
                choice[slot] = jnp.where(
                    jnp.logical_and(valid, lax.rem(entry, 9) == slot), jnp.int32(member), choice[slot]
                )

        def up_copy(index):
            return pltpu.make_async_remote_copy(
                src_ref=block_send.at[index],
                dst_ref=block_recv.at[1, index],
                send_sem=up_send_sem.at[index],
                recv_sem=up_recv_sem.at[index],
                device_id=(1 - sec, row, col),
                device_id_type=MESH,
            )

        def side_copy(index, step):
            lane_of = 0 if step < 0 else 1
            return pltpu.make_async_remote_copy(
                src_ref=block_recv.at[1, index],
                dst_ref=block_recv.at[1 - step, index],
                send_sem=side_send_sem.at[lane_of, index],
                recv_sem=side_recv_sem.at[lane_of, index],
                device_id=(sec, row + step, col),
                device_id_type=MESH,
            )

        for step in (-1, 1):

            @pl.when(jnp.logical_not(there(-step)))
            def _():
                block_recv[1 - step] = jnp.zeros(block_recv.shape[1:], jnp.float32)

        for index in range(count):
            up_copy(index).wait_recv()
            for step in (-1, 1):

                @pl.when(there(step))
                def _():
                    side_copy(index, step).start()

        for index in range(count):
            for step in (-1, 1):

                @pl.when(there(-step))
                def _():
                    side_copy(index, step).wait_recv()

            for slot in range(9):
                rows = slice((slot // 3) * patch_rows, (slot // 3 + 1) * patch_rows)
                lanes = slice((slot % 3) * patch_cols, (slot % 3 + 1) * patch_cols)
                own = ext[
                    1, index, top + rows.start : top + rows.stop, left + lanes.start : left + lanes.stop
                ]
                block = own
                for member in range(3):
                    block = jnp.where(choice[slot] == member, block_recv[member, index], block)
                out_ref[index, rows, lanes] = block

        for phase in range(2):
            for direction in range(8):

                @pl.when(there(*DIRECTIONS[direction]))
                def _():
                    halo_copy(phase, direction).wait_send()

        for member in range(3):

            @pl.when(there(member - 1))
            def _():
                rim_copy(member).wait_send()

        for index in range(count):
            for step in (-1, 1):

                @pl.when(there(step))
                def _():
                    side_copy(index, step).wait_send()

    @pl.when(is_nest)
    def _nest():
        load_force.wait()
        for now in range(2):
            ext[now, :, top - PAD_ROWS : top, left:right] = jnp.zeros((count, PAD_ROWS, width), jnp.float32)
            ext[now, :, bottom : bottom + PAD_ROWS, left:right] = jnp.zeros(
                (count, PAD_ROWS, width), jnp.float32
            )

        def bulk(index, carry):
            for substep in range(3):
                now = substep % 2

                def store(start, value, substep=substep, now=now):
                    if substep < 2:
                        ext[1 - now, index, top + start : top + start + chunk, left:right] = value
                    else:
                        out_ref[index, start : start + chunk] = value

                stencil_field(
                    index,
                    ext.at[now, index],
                    lambda start: 0.0,
                    lambda start: 0.0,
                    3.0 * diffusion[index],
                    third,
                    store,
                )
            return carry

        lax.fori_loop(0, count, bulk, 0)
        for member in range(3):

            @pl.when(there(member - 1))
            def _():
                pltpu.make_async_remote_copy(
                    src_ref=rim_send.at[2 - member],
                    dst_ref=rim_recv.at[member],
                    send_sem=rim_send_sem.at[2 - member],
                    recv_sem=rim_recv_sem.at[member],
                    device_id=(1 - sec, row + member - 1, col),
                    device_id_type=MESH,
                ).wait_recv()

            @pl.when(jnp.logical_not(there(member - 1)))
            def _():
                rim_recv[member] = jnp.zeros(rim_recv.shape[1:], jnp.float32)

        pick = lax.div(nest_patch[row, col], 9) - row + 1
        message = rim_recv[0]
        for member in (1, 2):
            message = jnp.where(pick == member, rim_recv[member], message)
        columns = message[16:32]

        def refine_weights(cells, fine, offset):
            nest = lax.broadcasted_iota(jnp.int32, (cells, fine), 1)
            cell = lax.broadcasted_iota(jnp.int32, (cells, fine), 0) - offset
            delta = nest - 3 * cell - 1
            near = jnp.abs(delta)
            value = jnp.where(near == 0, 3, jnp.where(near == 1, 2, jnp.where(near == 2, 1, 0)))
            return value.astype(jnp.float32)

        row_weights = refine_weights(LANES, width, 0)
        col_weights = refine_weights(LANES, height, PAD_ROWS)
        fine_rows = third * jnp.dot(
            message[0:16], row_weights, precision=lax.Precision.HIGHEST, preferred_element_type=jnp.float32
        )

        def corners(rows, at):
            west = columns[0:8, at : at + 1]
            east = columns[8:16, at : at + 1]
            return (
                rows
                + jnp.where(wide_lane == 0, third * west, 0.0)
                + jnp.where(wide_lane == width - 1, third * east, 0.0)
            )

        upper = corners(fine_rows[0:8], PAD_ROWS - 1)
        lower = corners(fine_rows[8:16], PAD_ROWS + patch_rows)
        column_block = jnp.concatenate([columns, jnp.zeros((LANES - 16, LANES), jnp.float32)], axis=0)
        fine_columns = third * jnp.dot(
            column_block, col_weights, precision=lax.Precision.HIGHEST, preferred_element_type=jnp.float32
        )
        tall = col_send.shape[-1]
        fine_columns = jnp.concatenate(
            [fine_columns, jnp.zeros((LANES, tall - height), jnp.float32)], axis=1
        )
        averaging = (
            lax.broadcasted_iota(jnp.int32, (width, patch_cols), 0) // 3
            == lax.broadcasted_iota(jnp.int32, (width, patch_cols), 1)
        ).astype(jnp.bfloat16)

        def strip(old, new, length, at_start, spread, outward, inward, before, after):
            shape = (8, old.shape[-1])
            line = lax.broadcasted_iota(jnp.int32, shape, 0)
            place = lax.broadcasted_iota(jnp.int32, shape, 1)
            edge, far = (0, 7) if at_start else (7, 0)
            toward, away = (1, 7) if at_start else (7, 1)
            value = jnp.zeros(shape, jnp.float32)
            for substep in range(3):
                rim = old + (substep / 3.0) * (new - old)
                outer = jnp.where(line == edge, rim, pltpu.roll(value, toward, 0))
                inner = jnp.where(line == far, 0.0, pltpu.roll(value, away, 0))
                previous = jnp.where(place == 0, 0.0, pltpu.roll(value, 1, 1))
                following = jnp.where(place == length - 1, 0.0, pltpu.roll(value, shape[1] - 1, 1))
                value = (
                    (1.0 - 4.0 * spread) * value
                    + outward * outer
                    + inward * inner
                    + before * previous
                    + after * following
                )
                value = jnp.where(place < length, value, 0.0)
            return value

        sides = [[], []]
        for index in range(count):
            spread = 3.0 * diffusion[index]
            north, south = spread + half_y, spread - half_y
            west, east = spread + half_x, spread - half_x
            at = 2 * index
            out_ref[index, 0:8] += strip(
                upper[at : at + 1], upper[at + 1 : at + 2], width, True, spread, north, south, west, east
            )
            out_ref[index, height - 8 : height] += strip(
                lower[at : at + 1], lower[at + 1 : at + 2], width, False, spread, south, north, west, east
            )
            for side in range(2):
                base = 8 * side + at
                near, beyond = (west, east) if side == 0 else (east, west)
                sides[side].append(
                    strip(
                        fine_columns[base : base + 1],
                        fine_columns[base + 1 : base + 2],
                        height,
                        side == 0,
                        spread,
                        near,
                        beyond,
                        north,
                        south,
                    )
                )
        stack = jnp.concatenate(
            sides[0] + sides[1] + [jnp.zeros((LANES - 16 * count, tall), jnp.float32)], axis=0
        ).T[0:height]
        for index in range(count):
            first = jnp.where(lane < 8, pltpu.roll(stack, (LANES - 8 * index) % LANES, 1), 0.0)
            shift = (LANES - 8 - 8 * count - 8 * index) % LANES
            last = jnp.where(lane >= LANES - 8, pltpu.roll(stack, shift, 1), 0.0)
            out_ref[index, :, 0:LANES] += first
            out_ref[index, :, width - LANES : width] += last
            full = out_ref[index]
            high = full.astype(jnp.bfloat16)
            low = (full - high.astype(jnp.float32)).astype(jnp.bfloat16)
            across = jnp.dot(high, averaging, preferred_element_type=jnp.float32) + jnp.dot(
                low, averaging, preferred_element_type=jnp.float32
            )
            fold[...] = across
            block_send[index] = (1.0 / 9.0) * (
                fold[pl.ds(0, patch_rows, stride=3)]
                + fold[pl.ds(1, patch_rows, stride=3)]
                + fold[pl.ds(2, patch_rows, stride=3)]
            )
            pltpu.make_async_remote_copy(
                src_ref=block_send.at[index],
                dst_ref=block_recv.at[1, index],
                send_sem=up_send_sem.at[index],
                recv_sem=up_recv_sem.at[index],
                device_id=(1 - sec, row, col),
                device_id_type=MESH,
            ).start()
        for index in range(count):
            pltpu.make_async_remote_copy(
                src_ref=block_send.at[index],
                dst_ref=block_recv.at[1, index],
                send_sem=up_send_sem.at[index],
                recv_sem=up_recv_sem.at[index],
                device_id=(1 - sec, row, col),
                device_id_type=MESH,
            ).wait_send()


def on_device(fields, forcing, courant, diffusion, nest_patch):
    _, count, levels, height, width = fields.shape
    own = fields.reshape(count, height, width)
    drive = forcing.reshape(count, height, width)
    rows_total = lax.axis_size("gy")
    cols_total = lax.axis_size("gx")
    patch_rows, patch_cols = height // 3, width // 3
    tall = -(-height // LANES) * LANES
    f32 = jnp.float32
    smem = pl.BlockSpec(memory_space=pltpu.SMEM)
    dma = pltpu.SemaphoreType.DMA
    result = pl.pallas_call(
        functools.partial(kernel, rows_total, cols_total),
        out_shape=jax.ShapeDtypeStruct((count, height, width), f32),
        in_specs=[pl.BlockSpec(memory_space=pl.ANY)] * 2 + [smem] * 3,
        out_specs=pl.BlockSpec(memory_space=pltpu.VMEM),
        scratch_shapes=[
            pltpu.VMEM((2, count, height + 2 * PAD_ROWS, width + 2 * LANES), f32),
            pltpu.VMEM((count, height, width), jnp.bfloat16),
            pltpu.VMEM((2, 2, 8, tall), f32),
            pltpu.VMEM((2, 2, 8, tall), f32),
            pltpu.VMEM((3, 16, width), f32),
            pltpu.VMEM((3, 32, LANES), f32),
            pltpu.VMEM((3, 32, LANES), f32),
            pltpu.VMEM((count, patch_rows, patch_cols), f32),
            pltpu.VMEM((3, count, patch_rows, patch_cols), f32),
            pltpu.VMEM((height, patch_cols), f32),
            dma((2,)),
            dma((2, 8)),
            dma((2, 8)),
            dma((3,)),
            dma((3,)),
            dma((count,)),
            dma((count,)),
            dma((2, count)),
            dma((2, count)),
        ],
        compiler_params=pltpu.CompilerParams(
            collective_id=0, has_side_effects=True, vmem_limit_bytes=40 * 1024 * 1024
        ),
    )(own, drive, courant, diffusion, nest_patch)
    return result.reshape(fields.shape)


def solution(mesh):
    return jax.shard_map(
        on_device,
        mesh=mesh,
        in_specs=(
            P("sec", None, None, "gy", "gx"),
            P("sec", None, None, "gy", "gx"),
            P(),
            P(),
            P(),
        ),
        out_specs=P("sec", None, None, "gy", "gx"),
        check_vma=False,
    )
```

```python
import functools

import jax
import jax.numpy as jnp
from jax import lax
from jax.experimental import pallas as pl
from jax.experimental.pallas import tpu as pltpu
from jax.sharding import PartitionSpec as P

MESH = pl.DeviceIdType.MESH
third = 1.0 / 3.0
PAD_ROWS = 8
LANES = 128
DIRECTIONS = ((-1, 0), (1, 0), (0, -1), (0, 1), (-1, -1), (-1, 1), (1, -1), (1, 1))


def all_of(terms):
    result = terms[0]
    for term in terms[1:]:
        result = jnp.logical_and(result, term)
    return result


def kernel(
    rows_total,
    cols_total,
    fields_hbm,
    forcing_hbm,
    courant,
    diffusion,
    nest_patch,
    out_ref,
    ext,
    force,
    col_send,
    col_recv,
    rim_rows,
    rim_send,
    rim_recv,
    block_send,
    block_recv,
    fold,
    ring_send,
    ring_recv,
    load_sem,
    halo_send_sem,
    halo_recv_sem,
    rim_send_sem,
    rim_recv_sem,
    up_send_sem,
    up_recv_sem,
    side_send_sem,
    side_recv_sem,
    ring_send_sem,
    ring_recv_sem,
):
    count, height, width = out_ref.shape
    patch_rows, patch_cols = height // 3, width // 3
    sec = lax.axis_index("sec")
    row = lax.axis_index("gy")
    col = lax.axis_index("gx")
    is_parent = sec == 0
    is_nest = sec == 1
    top, bottom = PAD_ROWS, PAD_ROWS + height
    left, right = LANES, LANES + width

    load_fields = pltpu.make_async_copy(
        fields_hbm, ext.at[0, :, top:bottom, left:right], load_sem.at[0]
    )
    load_force = pltpu.make_async_copy(forcing_hbm, force, load_sem.at[1])
    load_fields.start()
    load_force.start()

    def there(dy, dx=0):
        terms = []
        if dy < 0:
            terms.append(row > 0)
        if dy > 0:
            terms.append(row < rows_total - 1)
        if dx < 0:
            terms.append(col > 0)
        if dx > 0:
            terms.append(col < cols_total - 1)
        return all_of(terms) if terms else row >= 0

    barrier = pltpu.get_barrier_semaphore()

    def greet(condition, where):
        @pl.when(condition)
        def _():
            pl.semaphore_signal(barrier, inc=1, device_id=where, device_id_type=MESH)

    for dy, dx in DIRECTIONS:
        greet(all_of([is_parent, there(dy, dx)]), (sec, row + dy, col + dx))
    for dy in (-1, 0, 1):
        greet(there(dy), (1 - sec, row + dy, col))
    def one_if(condition):
        return jnp.where(condition, jnp.int32(1), jnp.int32(0))

    in_row = one_if(there(0, -1)) + one_if(there(0, 1)) + 1
    in_column = one_if(there(-1)) + one_if(there(1)) + 1
    pl.semaphore_wait(barrier, in_column + (1 - sec) * (in_row * in_column - 1))
    load_fields.wait()

    lane = lax.broadcasted_iota(jnp.int32, (1, LANES), 1)
    wide_lane = lax.broadcasted_iota(jnp.int32, (1, width), 1)
    half_x = 0.5 * courant[0, 0]
    half_y = 0.5 * courant[1, 0]
    chunk = 32

    def stencil_field(index, source, west_of, east_of, spread, drive_scale, store):
        for start in range(0, height, chunk):
            rows = slice(top + start, top + start + chunk)
            centre = source[rows, left:right]
            north = source[top + start - 1 : top + start - 1 + chunk, left:right]
            south = source[top + start + 1 : top + start + 1 + chunk, left:right]
            west = jnp.where(wide_lane == 0, west_of(start), pltpu.roll(centre, 1, 1))
            east = jnp.where(wide_lane == width - 1, east_of(start), pltpu.roll(centre, width - 1, 1))
            drive = force[index, start : start + chunk].astype(jnp.float32)
            value = (
                (1.0 - 4.0 * spread) * centre
                + (spread - half_x) * east
                + (spread + half_x) * west
                + (spread - half_y) * south
                + (spread + half_y) * north
                + drive_scale * drive
            )
            store(start, value)

    @pl.when(is_parent)
    def _parent():
        def halo_copy(phase, direction):
            dy, dx = DIRECTIONS[direction]
            where = (sec, row + dy, col + dx)
            sems = (halo_send_sem.at[phase, direction], halo_recv_sem.at[phase, direction])
            if dy == 0:
                side = 0 if dx < 0 else 1
                source = col_send.at[phase, side]
                target = col_recv.at[phase, 1 - side]
            else:
                rows_from = slice(top, top + PAD_ROWS) if dy < 0 else slice(bottom - PAD_ROWS, bottom)
                rows_to = slice(bottom, bottom + PAD_ROWS) if dy < 0 else slice(0, top)
                if dx == 0:
                    lanes_from = lanes_to = slice(left, right)
                elif dx < 0:
                    lanes_from, lanes_to = slice(left, left + LANES), slice(right, right + LANES)
                else:
                    lanes_from, lanes_to = slice(right - LANES, right), slice(0, left)
                source = ext.at[phase, :, rows_from, lanes_from]
                target = ext.at[phase, :, rows_to, lanes_to]
            return pltpu.make_async_remote_copy(
                src_ref=source,
                dst_ref=target,
                send_sem=sems[0],
                recv_sem=sems[1],
                device_id=where,
                device_id_type=MESH,
            )

        def start_exchange(phase):
            for direction in (0, 1, 4, 5, 6, 7):

                @pl.when(there(*DIRECTIONS[direction]))
                def _():
                    halo_copy(phase, direction).start()

            packed = jnp.zeros((height, LANES), jnp.float32)
            for index in range(count):
                first = ext[phase, index, top:bottom, left : left + LANES]
                last = ext[phase, index, top:bottom, right - LANES : right]
                packed = jnp.where(lane == index, first[:, 0:1], packed)
                packed = jnp.where(lane == 8 + index, last[:, LANES - 1 : LANES], packed)
            tall = col_send.shape[-1]
            packed = jnp.concatenate([packed, jnp.zeros((tall - height, LANES), jnp.float32)], axis=0)
            flat = packed.T
            col_send[phase, 0] = flat[0:8]
            col_send[phase, 1] = flat[8:16]
            for direction in (2, 3):

                @pl.when(there(*DIRECTIONS[direction]))
                def _():
                    halo_copy(phase, direction).start()

            for direction in range(8):
                dy, dx = DIRECTIONS[direction]

                @pl.when(jnp.logical_not(there(-dy, -dx)))
                def _():
                    if dy == 0:
                        side = 1 if dx < 0 else 0
                        col_recv[phase, side] = jnp.zeros(col_recv.shape[2:], jnp.float32)
                    else:
                        rows_to = slice(bottom, bottom + PAD_ROWS) if dy < 0 else slice(0, top)
                        if dx == 0:
                            lanes_to = slice(left, right)
                        elif dx < 0:
                            lanes_to = slice(right, right + LANES)
                        else:
                            lanes_to = slice(0, left)
                        ext[phase, :, rows_to, lanes_to] = jnp.zeros(
                            (count, PAD_ROWS, lanes_to.stop - lanes_to.start), jnp.float32
                        )

        def end_exchange(phase):
            for direction in range(8):
                dy, dx = DIRECTIONS[direction]

                @pl.when(there(-dy, -dx))
                def _():
                    halo_copy(phase, direction).wait_recv()

            both = jnp.concatenate(
                [
                    col_recv[phase, 0],
                    col_recv[phase, 1],
                    jnp.zeros((LANES - 16, col_recv.shape[-1]), jnp.float32),
                ],
                axis=0,
            )
            columns = both.T
            for index in range(count):
                for side, base in ((0, 0), (1, 8)):
                    value = columns[0:height, base + index : base + index + 1]
                    begin = 0 if side == 0 else right
                    ext[phase, index, top:bottom, begin : begin + LANES] = jnp.broadcast_to(
                        value, (height, LANES)
                    )

        start_exchange(0)
        load_force.wait()
        end_exchange(0)

        def advance(index, carry):
            source = ext.at[0, index]

            def store(start, value):
                ext[1, index, top + start : top + start + chunk, left:right] = value

            stencil_field(
                index,
                source,
                lambda start: source[top + start : top + start + chunk, 0:LANES][:, LANES - 1 : LANES],
                lambda start: source[top + start : top + start + chunk, right : right + LANES][:, 0:1],
                diffusion[index],
                1.0,
                store,
            )
            return carry

        lax.fori_loop(0, count, advance, 0)
        start_exchange(1)
        end_exchange(1)

        def rim_copy(member):
            return pltpu.make_async_remote_copy(
                src_ref=rim_send.at[member],
                dst_ref=rim_recv.at[2 - member],
                send_sem=rim_send_sem.at[member],
                recv_sem=rim_recv_sem.at[2 - member],
                device_id=(1 - sec, row + member - 1, col),
                device_id_type=MESH,
            )

        full = ext.shape[2]
        stretch = 2 * LANES
        packed = jnp.zeros((full, LANES), jnp.float32)
        for index in range(count):
            for phase in range(2):
                place = 2 * index + phase
                for part in range(3):
                    above = top + part * patch_rows - 1
                    below = top + (part + 1) * patch_rows
                    rim_rows[part, place : place + 1] = ext[phase, index, above : above + 1, left:right]
                    rim_rows[part, 8 + place : 9 + place] = ext[phase, index, below : below + 1, left:right]
                    begin = part * patch_cols
                    western = ext[phase, index, :, begin : begin + LANES]
                    begin = left + (part + 1) * patch_cols
                    eastern = ext[phase, index, :, begin : begin + LANES]
                    packed = jnp.where(lane == 16 * part + place, western[:, LANES - 1 : LANES], packed)
                    packed = jnp.where(lane == 16 * part + 8 + place, eastern[:, 0:1], packed)
        packed = jnp.concatenate([packed, jnp.zeros((stretch - full, LANES), jnp.float32)], axis=0)
        flat = packed.T

        def choose(number, options):
            return jnp.where(number == 0, options[0], jnp.where(number == 1, options[1], options[2]))

        for member in range(3):
            target_row = jnp.clip(row + member - 1, 0, rows_total - 1)
            slot = lax.rem(nest_patch[target_row, col], 9)
            slot_row = lax.div(slot, 3)
            slot_col = lax.rem(slot, 3)
            rows = choose(slot_row, [rim_rows[part] for part in range(3)])
            rim_send[member, 0:16] = choose(
                slot_col, [rows[:, part * patch_cols : (part + 1) * patch_cols] for part in range(3)]
            )
            lines = choose(slot_col, [flat[16 * part : 16 * part + 16] for part in range(3)])
            rim_send[member, 16:32] = choose(
                slot_row, [lines[:, part * patch_rows : part * patch_rows + LANES] for part in range(3)]
            )

            @pl.when(there(member - 1))
            def _():
                rim_copy(member).start()

        choice = [jnp.int32(-1)] * 9
        for member in range(3):
            source = row + member - 1
            entry = nest_patch[jnp.clip(source, 0, rows_total - 1), col]
            valid = all_of([source >= 0, source < rows_total, lax.div(entry, 9) == row])
            for slot in range(9):
                choice[slot] = jnp.where(
                    jnp.logical_and(valid, lax.rem(entry, 9) == slot), jnp.int32(member), choice[slot]
                )

        def up_copy(index):
            return pltpu.make_async_remote_copy(
                src_ref=block_send.at[index],
                dst_ref=block_recv.at[1, index],
                send_sem=up_send_sem.at[index],
                recv_sem=up_recv_sem.at[index],
                device_id=(1 - sec, row, col),
                device_id_type=MESH,
            )

        def side_copy(index, step):
            lane_of = 0 if step < 0 else 1
            return pltpu.make_async_remote_copy(
                src_ref=block_recv.at[1, index],
                dst_ref=block_recv.at[1 - step, index],
                send_sem=side_send_sem.at[lane_of, index],
                recv_sem=side_recv_sem.at[lane_of, index],
                device_id=(sec, row + step, col),
                device_id_type=MESH,
            )

        for step in (-1, 1):

            @pl.when(jnp.logical_not(there(-step)))
            def _():
                block_recv[1 - step] = jnp.zeros(block_recv.shape[1:], jnp.float32)
                ring_recv[1 - step] = jnp.zeros(ring_recv.shape[1:], jnp.float32)

        for index in range(count):
            up_copy(index).wait_recv()
            for step in (-1, 1):

                @pl.when(there(step))
                def _():
                    side_copy(index, step).start()

        def ring_side(step):
            lane_of = 1 if step < 0 else 2
            return pltpu.make_async_remote_copy(
                src_ref=ring_recv.at[1],
                dst_ref=ring_recv.at[1 - step],
                send_sem=ring_send_sem.at[lane_of],
                recv_sem=ring_recv_sem.at[lane_of],
                device_id=(sec, row + step, col),
                device_id_type=MESH,
            )

        pltpu.make_async_remote_copy(
            src_ref=ring_send,
            dst_ref=ring_recv.at[1],
            send_sem=ring_send_sem.at[0],
            recv_sem=ring_recv_sem.at[0],
            device_id=(1 - sec, row, col),
            device_id_type=MESH,
        ).wait_recv()
        for step in (-1, 1):

            @pl.when(there(step))
            def _():
                ring_side(step).start()

        for step in (-1, 1):

            @pl.when(there(-step))
            def _():
                ring_side(step).wait_recv()

        ring_columns = jnp.concatenate(
            [ring_recv[member, 8:16] for member in range(3)] + [jnp.zeros((LANES - 24, LANES), jnp.float32)],
            axis=0,
        ).T
        block_line = lax.broadcasted_iota(jnp.int32, (patch_rows, 1), 0)

        def corrected(member, index):
            at = 8 * member + index
            return (
                block_recv[member, index]
                + jnp.where(block_line == 0, ring_recv[member, index : index + 1], 0.0)
                + jnp.where(
                    block_line == patch_rows - 1,
                    ring_recv[member, count + index : count + index + 1],
                    0.0,
                )
                + jnp.where(lane == 0, ring_columns[0:patch_rows, at : at + 1], 0.0)
                + jnp.where(
                    lane == patch_cols - 1, ring_columns[0:patch_rows, at + count : at + count + 1], 0.0
                )
            )

        for index in range(count):
            for step in (-1, 1):

                @pl.when(there(-step))
                def _():
                    side_copy(index, step).wait_recv()

            candidates = [corrected(member, index) for member in range(3)]
            for slot in range(9):
                rows = slice((slot // 3) * patch_rows, (slot // 3 + 1) * patch_rows)
                lanes = slice((slot % 3) * patch_cols, (slot % 3 + 1) * patch_cols)
                own = ext[
                    1, index, top + rows.start : top + rows.stop, left + lanes.start : left + lanes.stop
                ]
                block = own
                for member in range(3):
                    block = jnp.where(choice[slot] == member, candidates[member], block)
                out_ref[index, rows, lanes] = block

        for phase in range(2):
            for direction in range(8):

                @pl.when(there(*DIRECTIONS[direction]))
                def _():
                    halo_copy(phase, direction).wait_send()

        for member in range(3):

            @pl.when(there(member - 1))
            def _():
                rim_copy(member).wait_send()

        for step in (-1, 1):

            @pl.when(there(step))
            def _():
                ring_side(step).wait_send()

        for index in range(count):
            for step in (-1, 1):

                @pl.when(there(step))
                def _():
                    side_copy(index, step).wait_send()

    @pl.when(is_nest)
    def _nest():
        load_force.wait()
        for now in range(2):
            ext[now, :, top - PAD_ROWS : top, left:right] = jnp.zeros((count, PAD_ROWS, width), jnp.float32)
            ext[now, :, bottom : bottom + PAD_ROWS, left:right] = jnp.zeros(
                (count, PAD_ROWS, width), jnp.float32
            )

        def bulk(index, carry):
            for substep in range(3):
                now = substep % 2

                def store(start, value, substep=substep, now=now):
                    if substep < 2:
                        ext[1 - now, index, top + start : top + start + chunk, left:right] = value
                    else:
                        out_ref[index, start : start + chunk] = value

                stencil_field(
                    index,
                    ext.at[now, index],
                    lambda start: 0.0,
                    lambda start: 0.0,
                    3.0 * diffusion[index],
                    third,
                    store,
                )
            return carry

        lax.fori_loop(0, count, bulk, 0)
        averaging = (
            lax.broadcasted_iota(jnp.int32, (width, patch_cols), 0) // 3
            == lax.broadcasted_iota(jnp.int32, (width, patch_cols), 1)
        ).astype(jnp.bfloat16)
        for index in range(count):
            full = out_ref[index]
            high = full.astype(jnp.bfloat16)
            low = (full - high.astype(jnp.float32)).astype(jnp.bfloat16)
            across = jnp.dot(high, averaging, preferred_element_type=jnp.float32) + jnp.dot(
                low, averaging, preferred_element_type=jnp.float32
            )
            fold[...] = across
            block_send[index] = (1.0 / 9.0) * (
                fold[pl.ds(0, patch_rows, stride=3)]
                + fold[pl.ds(1, patch_rows, stride=3)]
                + fold[pl.ds(2, patch_rows, stride=3)]
            )
            pltpu.make_async_remote_copy(
                src_ref=block_send.at[index],
                dst_ref=block_recv.at[1, index],
                send_sem=up_send_sem.at[index],
                recv_sem=up_recv_sem.at[index],
                device_id=(1 - sec, row, col),
                device_id_type=MESH,
            ).start()
        for member in range(3):

            @pl.when(there(member - 1))
            def _():
                pltpu.make_async_remote_copy(
                    src_ref=rim_send.at[2 - member],
                    dst_ref=rim_recv.at[member],
                    send_sem=rim_send_sem.at[2 - member],
                    recv_sem=rim_recv_sem.at[member],
                    device_id=(1 - sec, row + member - 1, col),
                    device_id_type=MESH,
                ).wait_recv()

            @pl.when(jnp.logical_not(there(member - 1)))
            def _():
                rim_recv[member] = jnp.zeros(rim_recv.shape[1:], jnp.float32)

        pick = lax.div(nest_patch[row, col], 9) - row + 1
        message = rim_recv[0]
        for member in (1, 2):
            message = jnp.where(pick == member, rim_recv[member], message)
        columns = message[16:32]

        def refine_weights(cells, fine, offset):
            nest = lax.broadcasted_iota(jnp.int32, (cells, fine), 1)
            cell = lax.broadcasted_iota(jnp.int32, (cells, fine), 0) - offset
            delta = nest - 3 * cell - 1
            near = jnp.abs(delta)
            value = jnp.where(near == 0, 3, jnp.where(near == 1, 2, jnp.where(near == 2, 1, 0)))
            return value.astype(jnp.float32)

        row_weights = refine_weights(LANES, width, 0)
        col_weights = refine_weights(LANES, height, PAD_ROWS)
        fine_rows = third * jnp.dot(
            message[0:16], row_weights, precision=lax.Precision.HIGHEST, preferred_element_type=jnp.float32
        )

        def corners(rows, at):
            west = columns[0:8, at : at + 1]
            east = columns[8:16, at : at + 1]
            return (
                rows
                + jnp.where(wide_lane == 0, third * west, 0.0)
                + jnp.where(wide_lane == width - 1, third * east, 0.0)
            )

        upper = corners(fine_rows[0:8], PAD_ROWS - 1)
        lower = corners(fine_rows[8:16], PAD_ROWS + patch_rows)
        column_block = jnp.concatenate([columns, jnp.zeros((LANES - 16, LANES), jnp.float32)], axis=0)
        fine_columns = third * jnp.dot(
            column_block, col_weights, precision=lax.Precision.HIGHEST, preferred_element_type=jnp.float32
        )
        tall = col_send.shape[-1]
        fine_columns = jnp.concatenate(
            [fine_columns, jnp.zeros((LANES, tall - height), jnp.float32)], axis=1
        )
        def strip(old, new, length, at_start, spread, outward, inward, before, after):
            shape = (8, old.shape[-1])
            line = lax.broadcasted_iota(jnp.int32, shape, 0)
            place = lax.broadcasted_iota(jnp.int32, shape, 1)
            edge, far = (0, 7) if at_start else (7, 0)
            toward, away = (1, 7) if at_start else (7, 1)
            value = jnp.zeros(shape, jnp.float32)
            for substep in range(3):
                rim = old + (substep / 3.0) * (new - old)
                outer = jnp.where(line == edge, rim, pltpu.roll(value, toward, 0))
                inner = jnp.where(line == far, 0.0, pltpu.roll(value, away, 0))
                previous = jnp.where(place == 0, 0.0, pltpu.roll(value, 1, 1))
                following = jnp.where(place == length - 1, 0.0, pltpu.roll(value, shape[1] - 1, 1))
                value = (
                    (1.0 - 4.0 * spread) * value
                    + outward * outer
                    + inward * inner
                    + before * previous
                    + after * following
                )
                value = jnp.where(place < length, value, 0.0)
            return value

        sides = [[], []]
        ring = [[], [], [], []]
        for index in range(count):
            spread = 3.0 * diffusion[index]
            north, south = spread + half_y, spread - half_y
            west, east = spread + half_x, spread - half_x
            at = 2 * index
            high_strip = strip(
                upper[at : at + 1], upper[at + 1 : at + 2], width, True, spread, north, south, west, east
            )
            low_strip = strip(
                lower[at : at + 1], lower[at + 1 : at + 2], width, False, spread, south, north, west, east
            )
            out_ref[index, 0:8] += high_strip
            out_ref[index, height - 8 : height] += low_strip
            ring[0].append(jnp.sum(high_strip, axis=0, keepdims=True))
            ring[1].append(jnp.sum(low_strip, axis=0, keepdims=True))
            for side in range(2):
                base = 8 * side + at
                near, beyond = (west, east) if side == 0 else (east, west)
                sides[side].append(
                    strip(
                        fine_columns[base : base + 1],
                        fine_columns[base + 1 : base + 2],
                        height,
                        side == 0,
                        spread,
                        near,
                        beyond,
                        north,
                        south,
                    )
                )
                ring[2 + side].append(jnp.sum(sides[side][-1], axis=0, keepdims=True))
        column_averaging = (
            lax.broadcasted_iota(jnp.int32, (tall, LANES), 0) // 3
            == lax.broadcasted_iota(jnp.int32, (tall, LANES), 1)
        ).astype(jnp.float32)
        for part, weigh in ((0, averaging.astype(jnp.float32)), (1, column_averaging)):
            ring_send[8 * part : 8 * part + 8] = (1.0 / 9.0) * jnp.dot(
                jnp.concatenate(ring[2 * part] + ring[2 * part + 1], axis=0),
                weigh,
                precision=lax.Precision.HIGHEST,
                preferred_element_type=jnp.float32,
            )
        ring_copy = pltpu.make_async_remote_copy(
            src_ref=ring_send,
            dst_ref=ring_recv.at[1],
            send_sem=ring_send_sem.at[0],
            recv_sem=ring_recv_sem.at[0],
            device_id=(1 - sec, row, col),
            device_id_type=MESH,
        )
        ring_copy.start()
        stack = jnp.concatenate(
            sides[0] + sides[1] + [jnp.zeros((LANES - 16 * count, tall), jnp.float32)], axis=0
        ).T[0:height]
        for index in range(count):
            first = jnp.where(lane < 8, pltpu.roll(stack, (LANES - 8 * index) % LANES, 1), 0.0)
            shift = (LANES - 8 - 8 * count - 8 * index) % LANES
            last = jnp.where(lane >= LANES - 8, pltpu.roll(stack, shift, 1), 0.0)
            out_ref[index, :, 0:LANES] += first
            out_ref[index, :, width - LANES : width] += last
        for index in range(count):
            pltpu.make_async_remote_copy(
                src_ref=block_send.at[index],
                dst_ref=block_recv.at[1, index],
                send_sem=up_send_sem.at[index],
                recv_sem=up_recv_sem.at[index],
                device_id=(1 - sec, row, col),
                device_id_type=MESH,
            ).wait_send()
        ring_copy.wait_send()


def on_device(fields, forcing, courant, diffusion, nest_patch):
    _, count, levels, height, width = fields.shape
    own = fields.reshape(count, height, width)
    drive = forcing.reshape(count, height, width)
    rows_total = lax.axis_size("gy")
    cols_total = lax.axis_size("gx")
    patch_rows, patch_cols = height // 3, width // 3
    tall = -(-height // LANES) * LANES
    f32 = jnp.float32
    smem = pl.BlockSpec(memory_space=pltpu.SMEM)
    dma = pltpu.SemaphoreType.DMA
    result = pl.pallas_call(
        functools.partial(kernel, rows_total, cols_total),
        out_shape=jax.ShapeDtypeStruct((count, height, width), f32),
        in_specs=[pl.BlockSpec(memory_space=pl.ANY)] * 2 + [smem] * 3,
        out_specs=pl.BlockSpec(memory_space=pltpu.VMEM),
        scratch_shapes=[
            pltpu.VMEM((2, count, height + 2 * PAD_ROWS, width + 2 * LANES), f32),
            pltpu.VMEM((count, height, width), jnp.bfloat16),
            pltpu.VMEM((2, 2, 8, tall), f32),
            pltpu.VMEM((2, 2, 8, tall), f32),
            pltpu.VMEM((3, 16, width), f32),
            pltpu.VMEM((3, 32, LANES), f32),
            pltpu.VMEM((3, 32, LANES), f32),
            pltpu.VMEM((count, patch_rows, patch_cols), f32),
            pltpu.VMEM((3, count, patch_rows, patch_cols), f32),
            pltpu.VMEM((height, patch_cols), f32),
            pltpu.VMEM((16, LANES), f32),
            pltpu.VMEM((3, 16, LANES), f32),
            dma((2,)),
            dma((2, 8)),
            dma((2, 8)),
            dma((3,)),
            dma((3,)),
            dma((count,)),
            dma((count,)),
            dma((2, count)),
            dma((2, count)),
            dma((3,)),
            dma((3,)),
        ],
        compiler_params=pltpu.CompilerParams(
            collective_id=0, has_side_effects=True, vmem_limit_bytes=40 * 1024 * 1024
        ),
    )(own, drive, courant, diffusion, nest_patch)
    return result.reshape(fields.shape)


def solution(mesh):
    return jax.shard_map(
        on_device,
        mesh=mesh,
        in_specs=(
            P("sec", None, None, "gy", "gx"),
            P("sec", None, None, "gy", "gx"),
            P(),
            P(),
            P(),
        ),
        out_specs=P("sec", None, None, "gy", "gx"),
        check_vma=False,
    )
```

```python
import functools

import jax
import jax.numpy as jnp
from jax import lax
from jax.experimental import pallas as pl
from jax.experimental.pallas import tpu as pltpu
from jax.sharding import PartitionSpec as P

MESH = pl.DeviceIdType.MESH
third = 1.0 / 3.0
PAD_ROWS = 8
LANES = 128
DIRECTIONS = ((-1, 0), (1, 0), (0, -1), (0, 1), (-1, -1), (-1, 1), (1, -1), (1, 1))


def all_of(terms):
    result = terms[0]
    for term in terms[1:]:
        result = jnp.logical_and(result, term)
    return result


def kernel(
    rows_total,
    cols_total,
    fields_hbm,
    forcing_hbm,
    courant,
    diffusion,
    nest_patch,
    out_ref,
    ext,
    force,
    col_send,
    col_recv,
    rim_rows,
    rim_send,
    rim_recv,
    block_send,
    block_recv,
    fold,
    ring_send,
    ring_recv,
    load_sem,
    halo_send_sem,
    halo_recv_sem,
    rim_send_sem,
    rim_recv_sem,
    up_send_sem,
    up_recv_sem,
    side_send_sem,
    side_recv_sem,
    ring_send_sem,
    ring_recv_sem,
):
    count, height, width = out_ref.shape
    patch_rows, patch_cols = height // 3, width // 3
    sec = lax.axis_index("sec")
    row = lax.axis_index("gy")
    col = lax.axis_index("gx")
    is_parent = sec == 0
    is_nest = sec == 1
    top, bottom = PAD_ROWS, PAD_ROWS + height
    left, right = LANES, LANES + width

    load_fields = pltpu.make_async_copy(
        fields_hbm, ext.at[0, :, top:bottom, left:right], load_sem.at[0]
    )
    load_force = pltpu.make_async_copy(forcing_hbm, force, load_sem.at[1])
    load_fields.start()
    load_force.start()

    def there(dy, dx=0):
        terms = []
        if dy < 0:
            terms.append(row > 0)
        if dy > 0:
            terms.append(row < rows_total - 1)
        if dx < 0:
            terms.append(col > 0)
        if dx > 0:
            terms.append(col < cols_total - 1)
        return all_of(terms) if terms else row >= 0

    barrier = pltpu.get_barrier_semaphore()

    def greet(condition, where):
        @pl.when(condition)
        def _():
            pl.semaphore_signal(barrier, inc=1, device_id=where, device_id_type=MESH)

    for dy, dx in DIRECTIONS:
        greet(all_of([is_parent, there(dy, dx)]), (sec, row + dy, col + dx))
    for dy in (-1, 0, 1):
        greet(there(dy), (1 - sec, row + dy, col))
    def one_if(condition):
        return jnp.where(condition, jnp.int32(1), jnp.int32(0))

    in_row = one_if(there(0, -1)) + one_if(there(0, 1)) + 1
    in_column = one_if(there(-1)) + one_if(there(1)) + 1
    pl.semaphore_wait(barrier, in_column + (1 - sec) * (in_row * in_column - 1))
    load_fields.wait()

    lane = lax.broadcasted_iota(jnp.int32, (1, LANES), 1)
    wide_lane = lax.broadcasted_iota(jnp.int32, (1, width), 1)
    half_x = 0.5 * courant[0, 0]
    half_y = 0.5 * courant[1, 0]
    chunk = 32

    def stencil_field(index, source, west_of, east_of, spread, drive_scale, store):
        for start in range(0, height, chunk):
            rows = slice(top + start, top + start + chunk)
            centre = source[rows, left:right]
            north = source[top + start - 1 : top + start - 1 + chunk, left:right]
            south = source[top + start + 1 : top + start + 1 + chunk, left:right]
            west = jnp.where(wide_lane == 0, west_of(start), pltpu.roll(centre, 1, 1))
            east = jnp.where(wide_lane == width - 1, east_of(start), pltpu.roll(centre, width - 1, 1))
            drive = force[index, start : start + chunk].astype(jnp.float32)
            value = (
                (1.0 - 4.0 * spread) * centre
                + (spread - half_x) * east
                + (spread + half_x) * west
                + (spread - half_y) * south
                + (spread + half_y) * north
                + drive_scale * drive
            )
            store(start, value)

    @pl.when(is_parent)
    def _parent():
        def halo_copy(phase, direction):
            dy, dx = DIRECTIONS[direction]
            where = (sec, row + dy, col + dx)
            sems = (halo_send_sem.at[phase, direction], halo_recv_sem.at[phase, direction])
            if dy == 0:
                side = 0 if dx < 0 else 1
                source = col_send.at[phase, side]
                target = col_recv.at[phase, 1 - side]
            else:
                rows_from = slice(top, top + PAD_ROWS) if dy < 0 else slice(bottom - PAD_ROWS, bottom)
                rows_to = slice(bottom, bottom + PAD_ROWS) if dy < 0 else slice(0, top)
                if dx == 0:
                    lanes_from = lanes_to = slice(left, right)
                elif dx < 0:
                    lanes_from, lanes_to = slice(left, left + LANES), slice(right, right + LANES)
                else:
                    lanes_from, lanes_to = slice(right - LANES, right), slice(0, left)
                source = ext.at[phase, :, rows_from, lanes_from]
                target = ext.at[phase, :, rows_to, lanes_to]
            return pltpu.make_async_remote_copy(
                src_ref=source,
                dst_ref=target,
                send_sem=sems[0],
                recv_sem=sems[1],
                device_id=where,
                device_id_type=MESH,
            )

        def start_exchange(phase):
            for direction in (0, 1, 4, 5, 6, 7):

                @pl.when(there(*DIRECTIONS[direction]))
                def _():
                    halo_copy(phase, direction).start()

            packed = jnp.zeros((height, LANES), jnp.float32)
            for index in range(count):
                first = ext[phase, index, top:bottom, left : left + LANES]
                last = ext[phase, index, top:bottom, right - LANES : right]
                packed = jnp.where(lane == index, first[:, 0:1], packed)
                packed = jnp.where(lane == 8 + index, last[:, LANES - 1 : LANES], packed)
            tall = col_send.shape[-1]
            packed = jnp.concatenate([packed, jnp.zeros((tall - height, LANES), jnp.float32)], axis=0)
            flat = packed.T
            col_send[phase, 0] = flat[0:8]
            col_send[phase, 1] = flat[8:16]
            for direction in (2, 3):

                @pl.when(there(*DIRECTIONS[direction]))
                def _():
                    halo_copy(phase, direction).start()

            for direction in range(8):
                dy, dx = DIRECTIONS[direction]

                @pl.when(jnp.logical_not(there(-dy, -dx)))
                def _():
                    if dy == 0:
                        side = 1 if dx < 0 else 0
                        col_recv[phase, side] = jnp.zeros(col_recv.shape[2:], jnp.float32)
                    else:
                        rows_to = slice(bottom, bottom + PAD_ROWS) if dy < 0 else slice(0, top)
                        if dx == 0:
                            lanes_to = slice(left, right)
                        elif dx < 0:
                            lanes_to = slice(right, right + LANES)
                        else:
                            lanes_to = slice(0, left)
                        ext[phase, :, rows_to, lanes_to] = jnp.zeros(
                            (count, PAD_ROWS, lanes_to.stop - lanes_to.start), jnp.float32
                        )

        def end_exchange(phase):
            for direction in range(8):
                dy, dx = DIRECTIONS[direction]

                @pl.when(there(-dy, -dx))
                def _():
                    halo_copy(phase, direction).wait_recv()

            both = jnp.concatenate(
                [
                    col_recv[phase, 0],
                    col_recv[phase, 1],
                    jnp.zeros((LANES - 16, col_recv.shape[-1]), jnp.float32),
                ],
                axis=0,
            )
            columns = both.T
            for index in range(count):
                for side, base in ((0, 0), (1, 8)):
                    value = columns[0:height, base + index : base + index + 1]
                    begin = 0 if side == 0 else right
                    ext[phase, index, top:bottom, begin : begin + LANES] = jnp.broadcast_to(
                        value, (height, LANES)
                    )

        start_exchange(0)
        load_force.wait()
        end_exchange(0)

        def advance(index, carry):
            source = ext.at[0, index]

            def store(start, value):
                ext[1, index, top + start : top + start + chunk, left:right] = value

            stencil_field(
                index,
                source,
                lambda start: source[top + start : top + start + chunk, 0:LANES][:, LANES - 1 : LANES],
                lambda start: source[top + start : top + start + chunk, right : right + LANES][:, 0:1],
                diffusion[index],
                1.0,
                store,
            )
            return carry

        lax.fori_loop(0, count, advance, 0)
        start_exchange(1)

        def rim_copy(member):
            return pltpu.make_async_remote_copy(
                src_ref=rim_send.at[member],
                dst_ref=rim_recv.at[2 - member],
                send_sem=rim_send_sem.at[member],
                recv_sem=rim_recv_sem.at[2 - member],
                device_id=(1 - sec, row + member - 1, col),
                device_id_type=MESH,
            )

        full = ext.shape[2]
        stretch = 2 * LANES

        def pack_rims(phase, packed):
            for index in range(count):
                place = 2 * index + phase
                for part in range(3):
                    above = top + part * patch_rows - 1
                    below = top + (part + 1) * patch_rows
                    rim_rows[part, place : place + 1] = ext[phase, index, above : above + 1, left:right]
                    rim_rows[part, 8 + place : 9 + place] = ext[phase, index, below : below + 1, left:right]
                    begin = part * patch_cols
                    western = ext[phase, index, :, begin : begin + LANES]
                    begin = left + (part + 1) * patch_cols
                    eastern = ext[phase, index, :, begin : begin + LANES]
                    packed = jnp.where(lane == 16 * part + place, western[:, LANES - 1 : LANES], packed)
                    packed = jnp.where(lane == 16 * part + 8 + place, eastern[:, 0:1], packed)
            return packed

        packed = pack_rims(0, jnp.zeros((full, LANES), jnp.float32))
        end_exchange(1)
        packed = pack_rims(1, packed)
        packed = jnp.concatenate([packed, jnp.zeros((stretch - full, LANES), jnp.float32)], axis=0)
        flat = packed.T

        def choose(number, options):
            return jnp.where(number == 0, options[0], jnp.where(number == 1, options[1], options[2]))

        for member in range(3):
            target_row = jnp.clip(row + member - 1, 0, rows_total - 1)
            slot = lax.rem(nest_patch[target_row, col], 9)
            slot_row = lax.div(slot, 3)
            slot_col = lax.rem(slot, 3)
            rows = choose(slot_row, [rim_rows[part] for part in range(3)])
            rim_send[member, 0:16] = choose(
                slot_col, [rows[:, part * patch_cols : (part + 1) * patch_cols] for part in range(3)]
            )
            lines = choose(slot_col, [flat[16 * part : 16 * part + 16] for part in range(3)])
            rim_send[member, 16:32] = choose(
                slot_row, [lines[:, part * patch_rows : part * patch_rows + LANES] for part in range(3)]
            )

            @pl.when(there(member - 1))
            def _():
                rim_copy(member).start()

        choice = [jnp.int32(-1)] * 9
        for member in range(3):
            source = row + member - 1
            entry = nest_patch[jnp.clip(source, 0, rows_total - 1), col]
            valid = all_of([source >= 0, source < rows_total, lax.div(entry, 9) == row])
            for slot in range(9):
                choice[slot] = jnp.where(
                    jnp.logical_and(valid, lax.rem(entry, 9) == slot), jnp.int32(member), choice[slot]
                )

        def up_copy(index):
            return pltpu.make_async_remote_copy(
                src_ref=block_send.at[index],
                dst_ref=block_recv.at[1, index],
                send_sem=up_send_sem.at[index],
                recv_sem=up_recv_sem.at[index],
                device_id=(1 - sec, row, col),
                device_id_type=MESH,
            )

        def side_copy(index, step):
            lane_of = 0 if step < 0 else 1
            return pltpu.make_async_remote_copy(
                src_ref=block_recv.at[1, index],
                dst_ref=block_recv.at[1 - step, index],
                send_sem=side_send_sem.at[lane_of, index],
                recv_sem=side_recv_sem.at[lane_of, index],
                device_id=(sec, row + step, col),
                device_id_type=MESH,
            )

        for step in (-1, 1):

            @pl.when(jnp.logical_not(there(-step)))
            def _():
                block_recv[1 - step] = jnp.zeros(block_recv.shape[1:], jnp.float32)
                ring_recv[1 - step] = jnp.zeros(ring_recv.shape[1:], jnp.float32)

        for index in range(count):
            up_copy(index).wait_recv()
            for step in (-1, 1):

                @pl.when(there(step))
                def _():
                    side_copy(index, step).start()

        def ring_side(step):
            lane_of = 1 if step < 0 else 2
            return pltpu.make_async_remote_copy(
                src_ref=ring_recv.at[1],
                dst_ref=ring_recv.at[1 - step],
                send_sem=ring_send_sem.at[lane_of],
                recv_sem=ring_recv_sem.at[lane_of],
                device_id=(sec, row + step, col),
                device_id_type=MESH,
            )

        pltpu.make_async_remote_copy(
            src_ref=ring_send,
            dst_ref=ring_recv.at[1],
            send_sem=ring_send_sem.at[0],
            recv_sem=ring_recv_sem.at[0],
            device_id=(1 - sec, row, col),
            device_id_type=MESH,
        ).wait_recv()
        for step in (-1, 1):

            @pl.when(there(step))
            def _():
                ring_side(step).start()

        for step in (-1, 1):

            @pl.when(there(-step))
            def _():
                ring_side(step).wait_recv()

        ring_columns = jnp.concatenate(
            [ring_recv[member, 8:16] for member in range(3)] + [jnp.zeros((LANES - 24, LANES), jnp.float32)],
            axis=0,
        ).T
        block_line = lax.broadcasted_iota(jnp.int32, (patch_rows, 1), 0)

        def corrected(member, index):
            at = 8 * member + index
            return (
                block_recv[member, index]
                + jnp.where(block_line == 0, ring_recv[member, index : index + 1], 0.0)
                + jnp.where(
                    block_line == patch_rows - 1,
                    ring_recv[member, count + index : count + index + 1],
                    0.0,
                )
                + jnp.where(lane == 0, ring_columns[0:patch_rows, at : at + 1], 0.0)
                + jnp.where(
                    lane == patch_cols - 1, ring_columns[0:patch_rows, at + count : at + count + 1], 0.0
                )
            )

        for index in range(count):
            for step in (-1, 1):

                @pl.when(there(-step))
                def _():
                    side_copy(index, step).wait_recv()

            candidates = [corrected(member, index) for member in range(3)]
            for slot in range(9):
                rows = slice((slot // 3) * patch_rows, (slot // 3 + 1) * patch_rows)
                lanes = slice((slot % 3) * patch_cols, (slot % 3 + 1) * patch_cols)
                own = ext[
                    1, index, top + rows.start : top + rows.stop, left + lanes.start : left + lanes.stop
                ]
                block = own
                for member in range(3):
                    block = jnp.where(choice[slot] == member, candidates[member], block)
                out_ref[index, rows, lanes] = block

        for phase in range(2):
            for direction in range(8):

                @pl.when(there(*DIRECTIONS[direction]))
                def _():
                    halo_copy(phase, direction).wait_send()

        for member in range(3):

            @pl.when(there(member - 1))
            def _():
                rim_copy(member).wait_send()

        for step in (-1, 1):

            @pl.when(there(step))
            def _():
                ring_side(step).wait_send()

        for index in range(count):
            for step in (-1, 1):

                @pl.when(there(step))
                def _():
                    side_copy(index, step).wait_send()

    @pl.when(is_nest)
    def _nest():
        load_force.wait()
        for now in range(2):
            ext[now, :, top - PAD_ROWS : top, left:right] = jnp.zeros((count, PAD_ROWS, width), jnp.float32)
            ext[now, :, bottom : bottom + PAD_ROWS, left:right] = jnp.zeros(
                (count, PAD_ROWS, width), jnp.float32
            )

        def bulk(index, carry):
            for substep in range(3):
                now = substep % 2

                def store(start, value, substep=substep, now=now):
                    if substep < 2:
                        ext[1 - now, index, top + start : top + start + chunk, left:right] = value
                    else:
                        out_ref[index, start : start + chunk] = value

                stencil_field(
                    index,
                    ext.at[now, index],
                    lambda start: 0.0,
                    lambda start: 0.0,
                    3.0 * diffusion[index],
                    third,
                    store,
                )
            return carry

        lax.fori_loop(0, count, bulk, 0)
        averaging = (
            lax.broadcasted_iota(jnp.int32, (width, patch_cols), 0) // 3
            == lax.broadcasted_iota(jnp.int32, (width, patch_cols), 1)
        ).astype(jnp.bfloat16)
        for index in range(count):
            full = out_ref[index]
            high = full.astype(jnp.bfloat16)
            low = (full - high.astype(jnp.float32)).astype(jnp.bfloat16)
            across = jnp.dot(high, averaging, preferred_element_type=jnp.float32) + jnp.dot(
                low, averaging, preferred_element_type=jnp.float32
            )
            fold[...] = across
            block_send[index] = (1.0 / 9.0) * (
                fold[pl.ds(0, patch_rows, stride=3)]
                + fold[pl.ds(1, patch_rows, stride=3)]
                + fold[pl.ds(2, patch_rows, stride=3)]
            )
            pltpu.make_async_remote_copy(
                src_ref=block_send.at[index],
                dst_ref=block_recv.at[1, index],
                send_sem=up_send_sem.at[index],
                recv_sem=up_recv_sem.at[index],
                device_id=(1 - sec, row, col),
                device_id_type=MESH,
            ).start()
        for member in range(3):

            @pl.when(there(member - 1))
            def _():
                pltpu.make_async_remote_copy(
                    src_ref=rim_send.at[2 - member],
                    dst_ref=rim_recv.at[member],
                    send_sem=rim_send_sem.at[2 - member],
                    recv_sem=rim_recv_sem.at[member],
                    device_id=(1 - sec, row + member - 1, col),
                    device_id_type=MESH,
                ).wait_recv()

            @pl.when(jnp.logical_not(there(member - 1)))
            def _():
                rim_recv[member] = jnp.zeros(rim_recv.shape[1:], jnp.float32)

        pick = lax.div(nest_patch[row, col], 9) - row + 1
        message = rim_recv[0]
        for member in (1, 2):
            message = jnp.where(pick == member, rim_recv[member], message)
        columns = message[16:32]

        def refine_weights(cells, fine, offset):
            nest = lax.broadcasted_iota(jnp.int32, (cells, fine), 1)
            cell = lax.broadcasted_iota(jnp.int32, (cells, fine), 0) - offset
            delta = nest - 3 * cell - 1
            near = jnp.abs(delta)
            value = jnp.where(near == 0, 3, jnp.where(near == 1, 2, jnp.where(near == 2, 1, 0)))
            return value.astype(jnp.float32)

        row_weights = refine_weights(LANES, width, 0)
        col_weights = refine_weights(LANES, height, PAD_ROWS)
        fine_rows = third * jnp.dot(
            message[0:16], row_weights, precision=lax.Precision.HIGHEST, preferred_element_type=jnp.float32
        )

        def corners(rows, at):
            west = columns[0:8, at : at + 1]
            east = columns[8:16, at : at + 1]
            return (
                rows
                + jnp.where(wide_lane == 0, third * west, 0.0)
                + jnp.where(wide_lane == width - 1, third * east, 0.0)
            )

        upper = corners(fine_rows[0:8], PAD_ROWS - 1)
        lower = corners(fine_rows[8:16], PAD_ROWS + patch_rows)
        column_block = jnp.concatenate([columns, jnp.zeros((LANES - 16, LANES), jnp.float32)], axis=0)
        fine_columns = third * jnp.dot(
            column_block, col_weights, precision=lax.Precision.HIGHEST, preferred_element_type=jnp.float32
        )
        tall = col_send.shape[-1]
        fine_columns = jnp.concatenate(
            [fine_columns, jnp.zeros((LANES, tall - height), jnp.float32)], axis=1
        )
        def strip(old, new, length, at_start, spread, outward, inward, before, after):
            shape = (8, old.shape[-1])
            line = lax.broadcasted_iota(jnp.int32, shape, 0)
            place = lax.broadcasted_iota(jnp.int32, shape, 1)
            edge, far = (0, 7) if at_start else (7, 0)
            toward, away = (1, 7) if at_start else (7, 1)
            value = jnp.zeros(shape, jnp.float32)
            for substep in range(3):
                rim = old + (substep / 3.0) * (new - old)
                outer = jnp.where(line == edge, rim, pltpu.roll(value, toward, 0))
                inner = jnp.where(line == far, 0.0, pltpu.roll(value, away, 0))
                previous = jnp.where(place == 0, 0.0, pltpu.roll(value, 1, 1))
                following = jnp.where(place == length - 1, 0.0, pltpu.roll(value, shape[1] - 1, 1))
                value = (
                    (1.0 - 4.0 * spread) * value
                    + outward * outer
                    + inward * inner
                    + before * previous
                    + after * following
                )
                value = jnp.where(place < length, value, 0.0)
            return value

        sides = [[], []]
        ring = [[], [], [], []]
        for index in range(count):
            spread = 3.0 * diffusion[index]
            north, south = spread + half_y, spread - half_y
            west, east = spread + half_x, spread - half_x
            at = 2 * index
            high_strip = strip(
                upper[at : at + 1], upper[at + 1 : at + 2], width, True, spread, north, south, west, east
            )
            low_strip = strip(
                lower[at : at + 1], lower[at + 1 : at + 2], width, False, spread, south, north, west, east
            )
            out_ref[index, 0:8] += high_strip
            out_ref[index, height - 8 : height] += low_strip
            ring[0].append(jnp.sum(high_strip, axis=0, keepdims=True))
            ring[1].append(jnp.sum(low_strip, axis=0, keepdims=True))
            for side in range(2):
                base = 8 * side + at
                near, beyond = (west, east) if side == 0 else (east, west)
                sides[side].append(
                    strip(
                        fine_columns[base : base + 1],
                        fine_columns[base + 1 : base + 2],
                        height,
                        side == 0,
                        spread,
                        near,
                        beyond,
                        north,
                        south,
                    )
                )
                ring[2 + side].append(jnp.sum(sides[side][-1], axis=0, keepdims=True))
        column_averaging = (
            lax.broadcasted_iota(jnp.int32, (tall, LANES), 0) // 3
            == lax.broadcasted_iota(jnp.int32, (tall, LANES), 1)
        ).astype(jnp.float32)
        for part, weigh in ((0, averaging.astype(jnp.float32)), (1, column_averaging)):
            ring_send[8 * part : 8 * part + 8] = (1.0 / 9.0) * jnp.dot(
                jnp.concatenate(ring[2 * part] + ring[2 * part + 1], axis=0),
                weigh,
                precision=lax.Precision.HIGHEST,
                preferred_element_type=jnp.float32,
            )
        ring_copy = pltpu.make_async_remote_copy(
            src_ref=ring_send,
            dst_ref=ring_recv.at[1],
            send_sem=ring_send_sem.at[0],
            recv_sem=ring_recv_sem.at[0],
            device_id=(1 - sec, row, col),
            device_id_type=MESH,
        )
        ring_copy.start()
        stack = jnp.concatenate(
            sides[0] + sides[1] + [jnp.zeros((LANES - 16 * count, tall), jnp.float32)], axis=0
        ).T[0:height]
        for index in range(count):
            first = jnp.where(lane < 8, pltpu.roll(stack, (LANES - 8 * index) % LANES, 1), 0.0)
            shift = (LANES - 8 - 8 * count - 8 * index) % LANES
            last = jnp.where(lane >= LANES - 8, pltpu.roll(stack, shift, 1), 0.0)
            out_ref[index, :, 0:LANES] += first
            out_ref[index, :, width - LANES : width] += last
        for index in range(count):
            pltpu.make_async_remote_copy(
                src_ref=block_send.at[index],
                dst_ref=block_recv.at[1, index],
                send_sem=up_send_sem.at[index],
                recv_sem=up_recv_sem.at[index],
                device_id=(1 - sec, row, col),
                device_id_type=MESH,
            ).wait_send()
        ring_copy.wait_send()


def on_device(fields, forcing, courant, diffusion, nest_patch):
    _, count, levels, height, width = fields.shape
    own = fields.reshape(count, height, width)
    drive = forcing.reshape(count, height, width)
    rows_total = lax.axis_size("gy")
    cols_total = lax.axis_size("gx")
    patch_rows, patch_cols = height // 3, width // 3
    tall = -(-height // LANES) * LANES
    f32 = jnp.float32
    smem = pl.BlockSpec(memory_space=pltpu.SMEM)
    dma = pltpu.SemaphoreType.DMA
    result = pl.pallas_call(
        functools.partial(kernel, rows_total, cols_total),
        out_shape=jax.ShapeDtypeStruct((count, height, width), f32),
        in_specs=[pl.BlockSpec(memory_space=pltpu.HBM)] * 2 + [smem] * 3,
        out_specs=pl.BlockSpec(memory_space=pltpu.VMEM),
        scratch_shapes=[
            pltpu.VMEM((2, count, height + 2 * PAD_ROWS, width + 2 * LANES), f32),
            pltpu.VMEM((count, height, width), jnp.bfloat16),
            pltpu.VMEM((2, 2, 8, tall), f32),
            pltpu.VMEM((2, 2, 8, tall), f32),
            pltpu.VMEM((3, 16, width), f32),
            pltpu.VMEM((3, 32, LANES), f32),
            pltpu.VMEM((3, 32, LANES), f32),
            pltpu.VMEM((count, patch_rows, patch_cols), f32),
            pltpu.VMEM((3, count, patch_rows, patch_cols), f32),
            pltpu.VMEM((height, patch_cols), f32),
            pltpu.VMEM((16, LANES), f32),
            pltpu.VMEM((3, 16, LANES), f32),
            dma((2,)),
            dma((2, 8)),
            dma((2, 8)),
            dma((3,)),
            dma((3,)),
            dma((count,)),
            dma((count,)),
            dma((2, count)),
            dma((2, count)),
            dma((3,)),
            dma((3,)),
        ],
        compiler_params=pltpu.CompilerParams(
            collective_id=0, has_side_effects=True, vmem_limit_bytes=63 * 1024 * 1024
        ),
    )(own, drive, courant, diffusion, nest_patch)
    return result.reshape(fields.shape)


def solution(mesh):
    return jax.shard_map(
        on_device,
        mesh=mesh,
        in_specs=(
            P("sec", None, None, "gy", "gx"),
            P("sec", None, None, "gy", "gx"),
            P(),
            P(),
            P(),
        ),
        out_specs=P("sec", None, None, "gy", "gx"),
        check_vma=False,
    )
```

```python
import functools

import jax
import jax.numpy as jnp
from jax import lax
from jax.experimental import pallas as pl
from jax.experimental.pallas import tpu as pltpu
from jax.sharding import PartitionSpec as P

MESH = pl.DeviceIdType.MESH
third = 1.0 / 3.0
PAD_ROWS = 8
LANES = 128
DIRECTIONS = ((-1, 0), (1, 0), (0, -1), (0, 1), (-1, -1), (-1, 1), (1, -1), (1, 1))


def all_of(terms):
    result = terms[0]
    for term in terms[1:]:
        result = jnp.logical_and(result, term)
    return result


def kernel(
    rows_total,
    cols_total,
    fields_hbm,
    forcing_hbm,
    courant,
    diffusion,
    nest_patch,
    out_ref,
    ext,
    force,
    col_send,
    col_recv,
    rim_rows,
    rim_send,
    rim_recv,
    block_send,
    block_recv,
    fold,
    ring_send,
    ring_recv,
    load_sem,
    halo_send_sem,
    halo_recv_sem,
    rim_send_sem,
    rim_recv_sem,
    up_send_sem,
    up_recv_sem,
    side_send_sem,
    side_recv_sem,
    ring_send_sem,
    ring_recv_sem,
):
    count, height, width = out_ref.shape
    patch_rows, patch_cols = height // 3, width // 3
    sec = lax.axis_index("sec")
    row = lax.axis_index("gy")
    col = lax.axis_index("gx")
    is_parent = sec == 0
    is_nest = sec == 1
    top, bottom = PAD_ROWS, PAD_ROWS + height
    left, right = LANES, LANES + width

    load_fields = pltpu.make_async_copy(
        fields_hbm, ext.at[0, :, top:bottom, left:right], load_sem.at[0]
    )
    load_force = pltpu.make_async_copy(forcing_hbm, force, load_sem.at[1])
    load_fields.start()
    load_force.start()

    def there(dy, dx=0):
        terms = []
        if dy < 0:
            terms.append(row > 0)
        if dy > 0:
            terms.append(row < rows_total - 1)
        if dx < 0:
            terms.append(col > 0)
        if dx > 0:
            terms.append(col < cols_total - 1)
        return all_of(terms) if terms else row >= 0

    barrier = pltpu.get_barrier_semaphore()

    def greet(condition, where):
        @pl.when(condition)
        def _():
            pl.semaphore_signal(barrier, inc=1, device_id=where, device_id_type=MESH)

    for dy, dx in DIRECTIONS:
        greet(all_of([is_parent, there(dy, dx)]), (sec, row + dy, col + dx))
    for dy in (-1, 0, 1):
        greet(there(dy), (1 - sec, row + dy, col))
    def one_if(condition):
        return jnp.where(condition, jnp.int32(1), jnp.int32(0))

    in_row = one_if(there(0, -1)) + one_if(there(0, 1)) + 1
    in_column = one_if(there(-1)) + one_if(there(1)) + 1
    pl.semaphore_wait(barrier, in_column + (1 - sec) * (in_row * in_column - 1))
    load_fields.wait()

    lane = lax.broadcasted_iota(jnp.int32, (1, LANES), 1)
    wide_lane = lax.broadcasted_iota(jnp.int32, (1, width), 1)
    half_x = 0.5 * courant[0]
    half_y = 0.5 * courant[1]
    chunk = 32

    def stencil_field(index, source, west_of, east_of, spread, drive_scale, store):
        for start in range(0, height, chunk):
            rows = slice(top + start, top + start + chunk)
            centre = source[rows, left:right]
            north = source[top + start - 1 : top + start - 1 + chunk, left:right]
            south = source[top + start + 1 : top + start + 1 + chunk, left:right]
            west = jnp.where(wide_lane == 0, west_of(start), pltpu.roll(centre, 1, 1))
            east = jnp.where(wide_lane == width - 1, east_of(start), pltpu.roll(centre, width - 1, 1))
            drive = force[index, start : start + chunk].astype(jnp.float32)
            value = (
                (1.0 - 4.0 * spread) * centre
                + (spread - half_x) * east
                + (spread + half_x) * west
                + (spread - half_y) * south
                + (spread + half_y) * north
                + drive_scale * drive
            )
            store(start, value)

    @pl.when(is_parent)
    def _parent():
        def halo_copy(phase, direction):
            dy, dx = DIRECTIONS[direction]
            where = (sec, row + dy, col + dx)
            sems = (halo_send_sem.at[phase, direction], halo_recv_sem.at[phase, direction])
            if dy == 0:
                side = 0 if dx < 0 else 1
                source = col_send.at[phase, side]
                target = col_recv.at[phase, 1 - side]
            else:
                rows_from = slice(top, top + PAD_ROWS) if dy < 0 else slice(bottom - PAD_ROWS, bottom)
                rows_to = slice(bottom, bottom + PAD_ROWS) if dy < 0 else slice(0, top)
                if dx == 0:
                    lanes_from = lanes_to = slice(left, right)
                elif dx < 0:
                    lanes_from, lanes_to = slice(left, left + LANES), slice(right, right + LANES)
                else:
                    lanes_from, lanes_to = slice(right - LANES, right), slice(0, left)
                source = ext.at[phase, :, rows_from, lanes_from]
                target = ext.at[phase, :, rows_to, lanes_to]
            return pltpu.make_async_remote_copy(
                src_ref=source,
                dst_ref=target,
                send_sem=sems[0],
                recv_sem=sems[1],
                device_id=where,
                device_id_type=MESH,
            )

        def start_exchange(phase):
            for direction in (0, 1, 4, 5, 6, 7):

                @pl.when(there(*DIRECTIONS[direction]))
                def _():
                    halo_copy(phase, direction).start()

            packed = jnp.zeros((height, LANES), jnp.float32)
            for index in range(count):
                first = ext[phase, index, top:bottom, left : left + LANES]
                last = ext[phase, index, top:bottom, right - LANES : right]
                packed = jnp.where(lane == index, first[:, 0:1], packed)
                packed = jnp.where(lane == 8 + index, last[:, LANES - 1 : LANES], packed)
            tall = col_send.shape[-1]
            packed = jnp.concatenate([packed, jnp.zeros((tall - height, LANES), jnp.float32)], axis=0)
            flat = packed.T
            col_send[phase, 0] = flat[0:8]
            col_send[phase, 1] = flat[8:16]
            for direction in (2, 3):

                @pl.when(there(*DIRECTIONS[direction]))
                def _():
                    halo_copy(phase, direction).start()

            for direction in range(8):
                dy, dx = DIRECTIONS[direction]

                @pl.when(jnp.logical_not(there(-dy, -dx)))
                def _():
                    if dy == 0:
                        side = 1 if dx < 0 else 0
                        col_recv[phase, side] = jnp.zeros(col_recv.shape[2:], jnp.float32)
                    else:
                        rows_to = slice(bottom, bottom + PAD_ROWS) if dy < 0 else slice(0, top)
                        if dx == 0:
                            lanes_to = slice(left, right)
                        elif dx < 0:
                            lanes_to = slice(right, right + LANES)
                        else:
                            lanes_to = slice(0, left)
                        ext[phase, :, rows_to, lanes_to] = jnp.zeros(
                            (count, PAD_ROWS, lanes_to.stop - lanes_to.start), jnp.float32
                        )

        def end_exchange(phase):
            for direction in range(8):
                dy, dx = DIRECTIONS[direction]

                @pl.when(there(-dy, -dx))
                def _():
                    halo_copy(phase, direction).wait_recv()

            both = jnp.concatenate(
                [
                    col_recv[phase, 0],
                    col_recv[phase, 1],
                    jnp.zeros((LANES - 16, col_recv.shape[-1]), jnp.float32),
                ],
                axis=0,
            )
            columns = both.T
            for index in range(count):
                for side, base in ((0, 0), (1, 8)):
                    value = columns[0:height, base + index : base + index + 1]
                    begin = 0 if side == 0 else right
                    ext[phase, index, top:bottom, begin : begin + LANES] = jnp.broadcast_to(
                        value, (height, LANES)
                    )

        start_exchange(0)
        load_force.wait()
        end_exchange(0)

        def advance(index, carry):
            source = ext.at[0, index]

            def store(start, value):
                ext[1, index, top + start : top + start + chunk, left:right] = value

            stencil_field(
                index,
                source,
                lambda start: source[top + start : top + start + chunk, 0:LANES][:, LANES - 1 : LANES],
                lambda start: source[top + start : top + start + chunk, right : right + LANES][:, 0:1],
                diffusion[index],
                1.0,
                store,
            )
            return carry

        lax.fori_loop(0, count, advance, 0)
        start_exchange(1)

        def rim_copy(member):
            return pltpu.make_async_remote_copy(
                src_ref=rim_send.at[member],
                dst_ref=rim_recv.at[2 - member],
                send_sem=rim_send_sem.at[member],
                recv_sem=rim_recv_sem.at[2 - member],
                device_id=(1 - sec, row + member - 1, col),
                device_id_type=MESH,
            )

        full = ext.shape[2]
        stretch = 2 * LANES

        def pack_rims(phase, packed):
            for index in range(count):
                place = 2 * index + phase
                for part in range(3):
                    above = top + part * patch_rows - 1
                    below = top + (part + 1) * patch_rows
                    rim_rows[part, place : place + 1] = ext[phase, index, above : above + 1, left:right]
                    rim_rows[part, 8 + place : 9 + place] = ext[phase, index, below : below + 1, left:right]
                    begin = part * patch_cols
                    western = ext[phase, index, :, begin : begin + LANES]
                    begin = left + (part + 1) * patch_cols
                    eastern = ext[phase, index, :, begin : begin + LANES]
                    packed = jnp.where(lane == 16 * part + place, western[:, LANES - 1 : LANES], packed)
                    packed = jnp.where(lane == 16 * part + 8 + place, eastern[:, 0:1], packed)
            return packed

        packed = pack_rims(0, jnp.zeros((full, LANES), jnp.float32))
        end_exchange(1)
        packed = pack_rims(1, packed)
        packed = jnp.concatenate([packed, jnp.zeros((stretch - full, LANES), jnp.float32)], axis=0)
        flat = packed.T

        def choose(number, options):
            return jnp.where(number == 0, options[0], jnp.where(number == 1, options[1], options[2]))

        for member in range(3):
            target_row = jnp.clip(row + member - 1, 0, rows_total - 1)
            slot = lax.rem(nest_patch[target_row, col], 9)
            slot_row = lax.div(slot, 3)
            slot_col = lax.rem(slot, 3)
            rows = choose(slot_row, [rim_rows[part] for part in range(3)])
            rim_send[member, 0:16] = choose(
                slot_col, [rows[:, part * patch_cols : (part + 1) * patch_cols] for part in range(3)]
            )
            lines = choose(slot_col, [flat[16 * part : 16 * part + 16] for part in range(3)])
            rim_send[member, 16:32] = choose(
                slot_row, [lines[:, part * patch_rows : part * patch_rows + LANES] for part in range(3)]
            )

            @pl.when(there(member - 1))
            def _():
                rim_copy(member).start()

        choice = [jnp.int32(-1)] * 9
        for member in range(3):
            source = row + member - 1
            entry = nest_patch[jnp.clip(source, 0, rows_total - 1), col]
            valid = all_of([source >= 0, source < rows_total, lax.div(entry, 9) == row])
            for slot in range(9):
                choice[slot] = jnp.where(
                    jnp.logical_and(valid, lax.rem(entry, 9) == slot), jnp.int32(member), choice[slot]
                )

        def up_copy(index):
            return pltpu.make_async_remote_copy(
                src_ref=block_send.at[index],
                dst_ref=block_recv.at[1, index],
                send_sem=up_send_sem.at[index],
                recv_sem=up_recv_sem.at[index],
                device_id=(1 - sec, row, col),
                device_id_type=MESH,
            )

        def side_copy(index, step):
            lane_of = 0 if step < 0 else 1
            return pltpu.make_async_remote_copy(
                src_ref=block_recv.at[1, index],
                dst_ref=block_recv.at[1 - step, index],
                send_sem=side_send_sem.at[lane_of, index],
                recv_sem=side_recv_sem.at[lane_of, index],
                device_id=(sec, row + step, col),
                device_id_type=MESH,
            )

        for step in (-1, 1):

            @pl.when(jnp.logical_not(there(-step)))
            def _():
                block_recv[1 - step] = jnp.zeros(block_recv.shape[1:], jnp.float32)
                ring_recv[1 - step] = jnp.zeros(ring_recv.shape[1:], jnp.float32)

        for index in range(count):
            up_copy(index).wait_recv()
            for step in (-1, 1):

                @pl.when(there(step))
                def _():
                    side_copy(index, step).start()

        def ring_side(step):
            lane_of = 1 if step < 0 else 2
            return pltpu.make_async_remote_copy(
                src_ref=ring_recv.at[1],
                dst_ref=ring_recv.at[1 - step],
                send_sem=ring_send_sem.at[lane_of],
                recv_sem=ring_recv_sem.at[lane_of],
                device_id=(sec, row + step, col),
                device_id_type=MESH,
            )

        pltpu.make_async_remote_copy(
            src_ref=ring_send,
            dst_ref=ring_recv.at[1],
            send_sem=ring_send_sem.at[0],
            recv_sem=ring_recv_sem.at[0],
            device_id=(1 - sec, row, col),
            device_id_type=MESH,
        ).wait_recv()
        for step in (-1, 1):

            @pl.when(there(step))
            def _():
                ring_side(step).start()

        for step in (-1, 1):

            @pl.when(there(-step))
            def _():
                ring_side(step).wait_recv()

        ring_columns = jnp.concatenate(
            [ring_recv[member, 8:16] for member in range(3)] + [jnp.zeros((LANES - 24, LANES), jnp.float32)],
            axis=0,
        ).T
        block_line = lax.broadcasted_iota(jnp.int32, (patch_rows, 1), 0)

        def corrected(member, index):
            at = 8 * member + index
            return (
                block_recv[member, index]
                + jnp.where(block_line == 0, ring_recv[member, index : index + 1], 0.0)
                + jnp.where(
                    block_line == patch_rows - 1,
                    ring_recv[member, count + index : count + index + 1],
                    0.0,
                )
                + jnp.where(lane == 0, ring_columns[0:patch_rows, at : at + 1], 0.0)
                + jnp.where(
                    lane == patch_cols - 1, ring_columns[0:patch_rows, at + count : at + count + 1], 0.0
                )
            )

        for index in range(count):
            for step in (-1, 1):

                @pl.when(there(-step))
                def _():
                    side_copy(index, step).wait_recv()

            candidates = [corrected(member, index) for member in range(3)]
            for slot in range(9):
                rows = slice((slot // 3) * patch_rows, (slot // 3 + 1) * patch_rows)
                lanes = slice((slot % 3) * patch_cols, (slot % 3 + 1) * patch_cols)
                own = ext[
                    1, index, top + rows.start : top + rows.stop, left + lanes.start : left + lanes.stop
                ]
                block = own
                for member in range(3):
                    block = jnp.where(choice[slot] == member, candidates[member], block)
                out_ref[index, rows, lanes] = block

        for phase in range(2):
            for direction in range(8):

                @pl.when(there(*DIRECTIONS[direction]))
                def _():
                    halo_copy(phase, direction).wait_send()

        for member in range(3):

            @pl.when(there(member - 1))
            def _():
                rim_copy(member).wait_send()

        for step in (-1, 1):

            @pl.when(there(step))
            def _():
                ring_side(step).wait_send()

        for index in range(count):
            for step in (-1, 1):

                @pl.when(there(step))
                def _():
                    side_copy(index, step).wait_send()

    @pl.when(is_nest)
    def _nest():
        load_force.wait()
        for now in range(2):
            ext[now, :, top - PAD_ROWS : top, left:right] = jnp.zeros((count, PAD_ROWS, width), jnp.float32)
            ext[now, :, bottom : bottom + PAD_ROWS, left:right] = jnp.zeros(
                (count, PAD_ROWS, width), jnp.float32
            )

        def bulk(index, carry):
            for substep in range(3):
                now = substep % 2

                def store(start, value, substep=substep, now=now):
                    if substep < 2:
                        ext[1 - now, index, top + start : top + start + chunk, left:right] = value
                    else:
                        out_ref[index, start : start + chunk] = value

                stencil_field(
                    index,
                    ext.at[now, index],
                    lambda start: 0.0,
                    lambda start: 0.0,
                    3.0 * diffusion[index],
                    third,
                    store,
                )
            return carry

        lax.fori_loop(0, count, bulk, 0)
        averaging = (
            lax.broadcasted_iota(jnp.int32, (width, patch_cols), 0) // 3
            == lax.broadcasted_iota(jnp.int32, (width, patch_cols), 1)
        ).astype(jnp.bfloat16)
        for index in range(count):
            full = out_ref[index]
            high = full.astype(jnp.bfloat16)
            low = (full - high.astype(jnp.float32)).astype(jnp.bfloat16)
            across = jnp.dot(high, averaging, preferred_element_type=jnp.float32) + jnp.dot(
                low, averaging, preferred_element_type=jnp.float32
            )
            fold[...] = across
            block_send[index] = (1.0 / 9.0) * (
                fold[pl.ds(0, patch_rows, stride=3)]
                + fold[pl.ds(1, patch_rows, stride=3)]
                + fold[pl.ds(2, patch_rows, stride=3)]
            )
            pltpu.make_async_remote_copy(
                src_ref=block_send.at[index],
                dst_ref=block_recv.at[1, index],
                send_sem=up_send_sem.at[index],
                recv_sem=up_recv_sem.at[index],
                device_id=(1 - sec, row, col),
                device_id_type=MESH,
            ).start()
        for member in range(3):

            @pl.when(there(member - 1))
            def _():
                pltpu.make_async_remote_copy(
                    src_ref=rim_send.at[2 - member],
                    dst_ref=rim_recv.at[member],
                    send_sem=rim_send_sem.at[2 - member],
                    recv_sem=rim_recv_sem.at[member],
                    device_id=(1 - sec, row + member - 1, col),
                    device_id_type=MESH,
                ).wait_recv()

            @pl.when(jnp.logical_not(there(member - 1)))
            def _():
                rim_recv[member] = jnp.zeros(rim_recv.shape[1:], jnp.float32)

        pick = lax.div(nest_patch[row, col], 9) - row + 1
        message = rim_recv[0]
        for member in (1, 2):
            message = jnp.where(pick == member, rim_recv[member], message)
        columns = message[16:32]

        def refine_weights(cells, fine, offset):
            nest = lax.broadcasted_iota(jnp.int32, (cells, fine), 1)
            cell = lax.broadcasted_iota(jnp.int32, (cells, fine), 0) - offset
            delta = nest - 3 * cell - 1
            near = jnp.abs(delta)
            value = jnp.where(near == 0, 3, jnp.where(near == 1, 2, jnp.where(near == 2, 1, 0)))
            return value.astype(jnp.float32)

        row_weights = refine_weights(LANES, width, 0)
        col_weights = refine_weights(LANES, height, PAD_ROWS)
        fine_rows = third * jnp.dot(
            message[0:16], row_weights, precision=lax.Precision.HIGHEST, preferred_element_type=jnp.float32
        )

        def corners(rows, at):
            west = columns[0:8, at : at + 1]
            east = columns[8:16, at : at + 1]
            return (
                rows
                + jnp.where(wide_lane == 0, third * west, 0.0)
                + jnp.where(wide_lane == width - 1, third * east, 0.0)
            )

        upper = corners(fine_rows[0:8], PAD_ROWS - 1)
        lower = corners(fine_rows[8:16], PAD_ROWS + patch_rows)
        column_block = jnp.concatenate([columns, jnp.zeros((LANES - 16, LANES), jnp.float32)], axis=0)
        fine_columns = third * jnp.dot(
            column_block, col_weights, precision=lax.Precision.HIGHEST, preferred_element_type=jnp.float32
        )
        tall = col_send.shape[-1]
        fine_columns = jnp.concatenate(
            [fine_columns, jnp.zeros((LANES, tall - height), jnp.float32)], axis=1
        )
        def strip(old, new, length, at_start, spread, outward, inward, before, after):
            shape = (8, old.shape[-1])
            line = lax.broadcasted_iota(jnp.int32, shape, 0)
            place = lax.broadcasted_iota(jnp.int32, shape, 1)
            edge, far = (0, 7) if at_start else (7, 0)
            toward, away = (1, 7) if at_start else (7, 1)
            value = jnp.zeros(shape, jnp.float32)
            for substep in range(3):
                rim = old + (substep / 3.0) * (new - old)
                outer = jnp.where(line == edge, rim, pltpu.roll(value, toward, 0))
                inner = jnp.where(line == far, 0.0, pltpu.roll(value, away, 0))
                previous = jnp.where(place == 0, 0.0, pltpu.roll(value, 1, 1))
                following = jnp.where(place == length - 1, 0.0, pltpu.roll(value, shape[1] - 1, 1))
                value = (
                    (1.0 - 4.0 * spread) * value
                    + outward * outer
                    + inward * inner
                    + before * previous
                    + after * following
                )
                value = jnp.where(place < length, value, 0.0)
            return value

        sides = [[], []]
        ring = [[], [], [], []]
        for index in range(count):
            spread = 3.0 * diffusion[index]
            north, south = spread + half_y, spread - half_y
            west, east = spread + half_x, spread - half_x
            at = 2 * index
            high_strip = strip(
                upper[at : at + 1], upper[at + 1 : at + 2], width, True, spread, north, south, west, east
            )
            low_strip = strip(
                lower[at : at + 1], lower[at + 1 : at + 2], width, False, spread, south, north, west, east
            )
            out_ref[index, 0:8] += high_strip
            out_ref[index, height - 8 : height] += low_strip
            ring[0].append(jnp.sum(high_strip, axis=0, keepdims=True))
            ring[1].append(jnp.sum(low_strip, axis=0, keepdims=True))
            for side in range(2):
                base = 8 * side + at
                near, beyond = (west, east) if side == 0 else (east, west)
                sides[side].append(
                    strip(
                        fine_columns[base : base + 1],
                        fine_columns[base + 1 : base + 2],
                        height,
                        side == 0,
                        spread,
                        near,
                        beyond,
                        north,
                        south,
                    )
                )
                ring[2 + side].append(jnp.sum(sides[side][-1], axis=0, keepdims=True))
        column_averaging = (
            lax.broadcasted_iota(jnp.int32, (tall, LANES), 0) // 3
            == lax.broadcasted_iota(jnp.int32, (tall, LANES), 1)
        ).astype(jnp.float32)
        for part, weigh in ((0, averaging.astype(jnp.float32)), (1, column_averaging)):
            ring_send[8 * part : 8 * part + 8] = (1.0 / 9.0) * jnp.dot(
                jnp.concatenate(ring[2 * part] + ring[2 * part + 1], axis=0),
                weigh,
                precision=lax.Precision.HIGHEST,
                preferred_element_type=jnp.float32,
            )
        ring_copy = pltpu.make_async_remote_copy(
            src_ref=ring_send,
            dst_ref=ring_recv.at[1],
            send_sem=ring_send_sem.at[0],
            recv_sem=ring_recv_sem.at[0],
            device_id=(1 - sec, row, col),
            device_id_type=MESH,
        )
        ring_copy.start()
        stack = jnp.concatenate(
            sides[0] + sides[1] + [jnp.zeros((LANES - 16 * count, tall), jnp.float32)], axis=0
        ).T[0:height]
        for index in range(count):
            first = jnp.where(lane < 8, pltpu.roll(stack, (LANES - 8 * index) % LANES, 1), 0.0)
            shift = (LANES - 8 - 8 * count - 8 * index) % LANES
            last = jnp.where(lane >= LANES - 8, pltpu.roll(stack, shift, 1), 0.0)
            out_ref[index, :, 0:LANES] += first
            out_ref[index, :, width - LANES : width] += last
        for index in range(count):
            pltpu.make_async_remote_copy(
                src_ref=block_send.at[index],
                dst_ref=block_recv.at[1, index],
                send_sem=up_send_sem.at[index],
                recv_sem=up_recv_sem.at[index],
                device_id=(1 - sec, row, col),
                device_id_type=MESH,
            ).wait_send()
        ring_copy.wait_send()


def on_device(fields, forcing, courant, diffusion, nest_patch):
    _, count, levels, height, width = fields.shape
    own = fields.reshape(count, height, width)
    drive = forcing.reshape(count, height, width)
    rows_total = lax.axis_size("gy")
    cols_total = lax.axis_size("gx")
    patch_rows, patch_cols = height // 3, width // 3
    tall = -(-height // LANES) * LANES
    f32 = jnp.float32
    smem = pl.BlockSpec(memory_space=pltpu.SMEM)
    dma = pltpu.SemaphoreType.DMA
    result = pl.pallas_call(
        functools.partial(kernel, rows_total, cols_total),
        out_shape=jax.ShapeDtypeStruct((count, height, width), f32),
        in_specs=[pl.BlockSpec(memory_space=pltpu.HBM)] * 2 + [smem] * 3,
        out_specs=pl.BlockSpec(memory_space=pltpu.VMEM),
        scratch_shapes=[
            pltpu.VMEM((2, count, height + 2 * PAD_ROWS, width + 2 * LANES), f32),
            pltpu.VMEM((count, height, width), jnp.bfloat16),
            pltpu.VMEM((2, 2, 8, tall), f32),
            pltpu.VMEM((2, 2, 8, tall), f32),
            pltpu.VMEM((3, 16, width), f32),
            pltpu.VMEM((3, 32, LANES), f32),
            pltpu.VMEM((3, 32, LANES), f32),
            pltpu.VMEM((count, patch_rows, patch_cols), f32),
            pltpu.VMEM((3, count, patch_rows, patch_cols), f32),
            pltpu.VMEM((height, patch_cols), f32),
            pltpu.VMEM((16, LANES), f32),
            pltpu.VMEM((3, 16, LANES), f32),
            dma((2,)),
            dma((2, 8)),
            dma((2, 8)),
            dma((3,)),
            dma((3,)),
            dma((count,)),
            dma((count,)),
            dma((2, count)),
            dma((2, count)),
            dma((3,)),
            dma((3,)),
        ],
        compiler_params=pltpu.CompilerParams(
            collective_id=0, has_side_effects=True, vmem_limit_bytes=63 * 1024 * 1024
        ),
    )(own, drive, courant.reshape(2), diffusion, nest_patch)
    return result.reshape(fields.shape)


def solution(mesh):
    return jax.shard_map(
        on_device,
        mesh=mesh,
        in_specs=(
            P("sec", None, None, "gy", "gx"),
            P("sec", None, None, "gy", "gx"),
            P(),
            P(),
            P(),
        ),
        out_specs=P("sec", None, None, "gy", "gx"),
        check_vma=False,
    )
```
